128 devices in a mesh: ctx: 32 (over z, x_lo, y), tp: 4 (over x_hi, core).
Axes of the slice: x: 4 (x_hi: 2, x_lo: 2; x = x_hi * 2 + x_lo), y: 4, z: 4, core: 2. Of those that a mesh axis runs over, the one named last changes fastest.
Arguments:
- q_self: bfloat16 [6144, 2560], P('ctx', 'tp'), may hold values from -64 to 64
- k_self: bfloat16 [6144, 2560], P('ctx', 'tp'), may hold values from -64 to 64
- v_self: bfloat16 [6144, 2560], P('ctx', 'tp'), may hold values from -6 to 6
- grad_self: bfloat16 [6144, 2560], P('ctx', 'tp'), may hold values from -448 to 448
- q_cross: bfloat16 [6144, 2560], P('ctx', 'tp'), may hold values from -64 to 64
- grad_cross: bfloat16 [6144, 2560], P('ctx', 'tp'), may hold values from -80 to 80
- k_text: bfloat16 [512, 2560], P(None, 'tp'), may hold values from -64 to 64
- v_text: bfloat16 [512, 2560], P(None, 'tp'), may hold values from -6 to 6
- gain_q: float32 [2560], P('tp'), may hold values from 0.1 to 1.9
- gain_k: float32 [2560], P('tp'), may hold values from 0.1 to 1.9
- gain_cross_q: float32 [2560], P('tp'), may hold values from 0.1 to 1.9
- gain_text_k: float32 [2560], P('tp'), may hold values from 0.1 to 1.9
Outputs:
- grad_q_self: bfloat16 [6144, 2560], P('ctx', 'tp')
- grad_k_self: bfloat16 [6144, 2560], P('ctx', 'tp')
- grad_v_self: bfloat16 [6144, 2560], P('ctx', 'tp')
- grad_q_cross: bfloat16 [6144, 2560], P('ctx', 'tp')
- grad_k_text: bfloat16 [512, 2560], P(None, 'tp')
- grad_v_text: bfloat16 [512, 2560], P(None, 'tp')
The draws below stay inside these ranges and needn't reach their ends.
All inputs are finite; a program needn't handle non-finite values.
Results may differ from the reference program's by a relative error of at most 0.034.
Values may be sent and summed in bfloat16 or wider, within the bound.
No kernel may reach another device: no remote copies, remote signals or barrier semaphores. Data moves between devices by JAX's collectives and lax.ppermute only.
A program may use at most 192 MiB of HBM per device.

```python
import math
import jax
import jax.numpy as jnp
from jax import lax

HD = 128
TEXT = 512
TOK_DEV = 192
TOKENS = 6144
HEADS = 20


def rough_rows(key, row_count):
    features = HEADS * HD
    key_entries, key_rowscale = jax.random.split(key, 2)
    column = jnp.arange(features, dtype=jnp.float32)
    entries = jnp.clip(jax.random.normal(key_entries, (row_count, features), jnp.float32), -4.0, 4.0)
    row_scale = jnp.exp(jax.random.uniform(key_rowscale, (row_count, 1), jnp.float32) * math.log(4.0))
    ramp_up = jnp.exp(column / (features - 1) * 0.5 * math.log(3.0))
    return entries * row_scale * ramp_up


def pair_draw(key, rows_query, rows_key):
    key_query, key_keys = jax.random.split(key, 2)
    queries = rough_rows(key_query, rows_query)
    key_rows = rough_rows(key_keys, rows_key)
    return (queries, key_rows)


def draw_q_self(key, part):
    return pair_draw(jax.random.fold_in(key, 101), TOKENS, TOKENS)[0].astype(jnp.bfloat16)


def draw_k_self(key, part):
    return pair_draw(jax.random.fold_in(key, 101), TOKENS, TOKENS)[1].astype(jnp.bfloat16)


def draw_q_cross(key, part):
    return pair_draw(jax.random.fold_in(key, 202), TOKENS, TEXT)[0].astype(jnp.bfloat16)


def draw_k_text(key, part):
    return pair_draw(jax.random.fold_in(key, 202), TOKENS, TEXT)[1].astype(jnp.bfloat16)


def block_levels(rng, extent, cuts, smallest, largest):
    loudness = 1.0
    for axis_at, parts in cuts:
        draws = jax.random.uniform(jax.random.fold_in(jax.random.fold_in(rng, 6), axis_at), (parts,), jnp.float32, smallest / len(cuts), largest / len(cuts))
        loudness = loudness * jnp.repeat(jnp.exp(draws), extent[axis_at] // parts).reshape((-1,) + (1,) * (len(extent) - 1 - axis_at))
    return loudness


def scatter_about(own_key, extent, spread, reach, cuts=(), kind=jnp.bfloat16):
    values = jax.random.normal(own_key, extent, jnp.float32) * spread
    if len(cuts) > 0:
        values = block_levels(own_key, extent, cuts, -0.22, 0.18) * values
    return jnp.clip(values, min=-reach, max=reach).astype(kind)


def setup_inputs(seed: int = 0) -> dict:
    key_of = jax.random.split(jax.random.key(seed), 13)
    q_self = draw_q_self(jax.random.fold_in(key_of[12], 71), 0)
    k_self = draw_k_self(jax.random.fold_in(key_of[12], 71), 0)
    v_self = scatter_about(key_of[2], (TOKENS, HEADS * HD), 1.0, 6.0, ((0, 32), (1, 4)))
    grad_self = scatter_about(key_of[3], (TOKENS, HEADS * HD), (TOKENS ** 0.5), 448.0, ((0, 32), (1, 4)))
    q_cross = draw_q_cross(jax.random.fold_in(key_of[12], 71), 0)
    grad_cross = scatter_about(key_of[5], (TOKENS, HEADS * HD), (2 * TEXT / TOKENS ** 0.5), 80.0, ((0, 32), (1, 4)))
    k_text = draw_k_text(jax.random.fold_in(key_of[12], 71), 0)
    v_text = scatter_about(key_of[7], (TEXT, HEADS * HD), 1.0, 6.0, ((1, 4),))
    gain_q = jnp.clip(1.0 + 0.18 * jax.random.normal(key_of[8], (HEADS * HD,), jnp.float32), 0.1, 1.9)
    gain_k = jnp.clip(1.0 + 0.18 * jax.random.normal(key_of[9], (HEADS * HD,), jnp.float32), 0.1, 1.9)
    gain_cross_q = jnp.clip(1.0 + 0.18 * jax.random.normal(key_of[10], (HEADS * HD,), jnp.float32), 0.1, 1.9)
    gain_text_k = jnp.clip(1.0 + 0.18 * jax.random.normal(key_of[11], (HEADS * HD,), jnp.float32), 0.1, 1.9)
    return dict(q_self=q_self, k_self=k_self, v_self=v_self, grad_self=grad_self, q_cross=q_cross, grad_cross=grad_cross, k_text=k_text, v_text=v_text, gain_q=gain_q, gain_k=gain_k, gain_cross_q=gain_cross_q, gain_text_k=gain_text_k)


epsilon = 1e-06

def normalize(tensor, gain):
    floats = tensor.astype(jnp.float32)
    inverse = lax.rsqrt(lax.optimization_barrier(jnp.mean(floats * floats, axis=1, keepdims=True)) + epsilon)
    return ((floats * inverse * gain).astype(jnp.bfloat16), inverse)

def norm_grad(tensor, inverse, gain, gradient):
    unit_rows = tensor.astype(jnp.float32) * inverse
    scaled = gradient * gain
    middle = lax.optimization_barrier(jnp.mean(scaled * unit_rows, axis=1, keepdims=True))
    return (inverse * (scaled - unit_rows * middle)).astype(jnp.bfloat16)

def split_heads(tensor):
    return tensor.astype(jnp.float32).reshape(tensor.shape[0], -1, HD)

def rounded(tensor):
    return lax.optimization_barrier(tensor.astype(jnp.bfloat16)).astype(jnp.float32)

def attend_back(queries, key_rows, values, grad_out):
    query_heads = split_heads(queries)
    key_heads = split_heads(key_rows)
    value_heads = split_heads(values)
    grad_heads = split_heads(grad_out)
    scaling = HD ** (-0.5)
    scores = jnp.einsum('qhd,khd->hqk', query_heads, key_heads) * scaling
    maximum = lax.optimization_barrier(jnp.max(scores, axis=2, keepdims=True))
    weights = jnp.exp(scores - maximum)
    totals = lax.optimization_barrier(jnp.sum(weights, axis=2, keepdims=True))
    grad_prob = jnp.einsum('qhd,khd->hqk', grad_heads, value_heads)
    deltas = lax.optimization_barrier(jnp.sum(weights * grad_prob, axis=2, keepdims=True)) / totals
    probability = weights / totals
    grad_score = rounded(probability * (grad_prob - deltas))
    grad_query = jnp.einsum('hqk,khd->qhd', grad_score, key_heads) * scaling
    grad_keys = jnp.einsum('hqk,qhd->khd', grad_score, query_heads) * scaling
    grad_values = jnp.einsum('hqk,qhd->khd', rounded(probability), grad_heads)
    return (grad_query.reshape(queries.shape[0], -1), grad_keys.reshape(key_rows.shape[0], -1), grad_values.reshape(key_rows.shape[0], -1))

def attention_grads(queries, key_rows, values, grad_out):
    block_count = queries.shape[0] // TOK_DEV
    query_blocks = queries.reshape(block_count, TOK_DEV, -1)
    grad_blocks = grad_out.reshape(block_count, TOK_DEV, -1)

    def advance(running, blocks):
        terms = attend_back(blocks[0], key_rows, values, blocks[1])
        return ((running[0] + terms[1], running[1] + terms[2]), terms[0])
    empty = jnp.zeros(key_rows.shape, jnp.float32)
    sums, query_terms = lax.scan(advance, (empty, empty), (query_blocks, grad_blocks))
    return (query_terms.reshape(queries.shape[0], -1), sums[0], sums[1])

def reference(q_self, k_self, v_self, grad_self, q_cross, grad_cross, k_text, v_text, gain_q, gain_k, gain_cross_q, gain_text_k):
    query_norm, inverse_q = normalize(q_self, gain_q)
    key_norm, inverse_k = normalize(k_self, gain_k)
    cross_norm, inverse_c = normalize(q_cross, gain_cross_q)
    text_norm, inverse_t = normalize(k_text, gain_text_k)
    grad_query, grad_key, grad_value = attention_grads(query_norm, key_norm, v_self, grad_self)
    grad_crossq, text_key, text_value = attention_grads(cross_norm, text_norm, v_text, grad_cross)
    return (norm_grad(q_self, inverse_q, gain_q, grad_query), norm_grad(k_self, inverse_k, gain_k, grad_key), grad_value.astype(jnp.bfloat16), norm_grad(q_cross, inverse_c, gain_cross_q, grad_crossq), norm_grad(k_text, inverse_t, gain_text_k, text_key), text_value.astype(jnp.bfloat16))
```

```python
import math

import jax
import jax.numpy as jnp
from jax import lax
from jax.experimental import pallas as pl
from jax.experimental.pallas import tpu as pltpu
from jax.sharding import Mesh, PartitionSpec as P

HD = 128
ROWS = 192
FEATURES = 2560
HEADS_DEV = 5
SHARED = HEADS_DEV - 1
BLOCK = 4 * ROWS
TEXT = 512
EPS = 1e-6
SCALE = HD ** (-0.5)
FOLD = SCALE * math.log2(math.e)
LN2 = math.log(2.0)
F32 = jnp.float32
BF16 = jnp.bfloat16
NT = (((1,), (1,)), ((), ()))
NN = (((1,), (0,)), ((), ()))

VMEM = pl.BlockSpec(memory_space=pltpu.VMEM)
SMEM = pl.BlockSpec(memory_space=pltpu.SMEM)


def shape(dims, dtype=BF16):
    return jax.ShapeDtypeStruct(dims, dtype)


def call(kernel, outs, index, arrays, scratch=(), flops=0, moved=0):
    single = not isinstance(outs, (list, tuple))
    return pl.pallas_call(
        kernel,
        out_shape=outs,
        in_specs=[SMEM] + [VMEM] * len(arrays),
        out_specs=VMEM if single else [VMEM] * len(outs),
        scratch_shapes=list(scratch),
        compiler_params=pltpu.CompilerParams(vmem_limit_bytes=56 * 2**20),
        cost_estimate=pl.CostEstimate(flops=flops, bytes_accessed=moved, transcendentals=0),
    )(index, *arrays)


def dot(a, b, dims):
    return lax.dot_general(a, b, dims, preferred_element_type=F32)


def along_lanes(tile):
    return jnp.sum(tile.T, axis=0, keepdims=True)


def along_rows(row):
    return jnp.broadcast_to(row, (HD, row.shape[1])).T


def inverse_of(square_sum):
    return lax.rsqrt(square_sum / FEATURES + EPS)


def head_at(ref, head):
    start = head * HD
    if not isinstance(head, int):
        start = pl.multiple_of(start, HD)
    return ref[:, pl.ds(start, HD)]


def square_rows(ref):
    tile = None
    for head in range(HEADS_DEV):
        part = head_at(ref, head).astype(F32)
        tile = part * part if tile is None else tile + part * part
    return along_lanes(tile)


def prepare_kernel(index, q, k, v, do, qc, kt, sums, a0, a1, a2, a3, b0, b1, b2, b3):
    sums[...] = jnp.zeros_like(sums)
    sums[0:1, 0:ROWS] = square_rows(q)
    sums[1:2, 0:ROWS] = square_rows(k)
    sums[2:3, 0:ROWS] = square_rows(qc)
    sums[3:4, :] = square_rows(kt)
    for d, (a, b) in enumerate(((a0, b0), (a1, b1), (a2, b2), (a3, b3))):
        head = lax.rem(index[0] + d, 4)
        a[0] = head_at(q, head)
        a[1] = head_at(do, head)
        b[0] = head_at(k, head)
        b[1] = head_at(v, head)
        b[2] = head_at(k, SHARED)
        b[3] = head_at(v, SHARED)


def norm_queries_kernel(index, t0, t1, t2, t3, a0, a1, a2, a3, q, do, gain, out):
    head = index[0]
    weight = head_at(gain, head) * FOLD
    for d, (t, a) in enumerate(((t0, a0), (t1, a1), (t2, a2), (t3, a3))):
        inv = along_rows(inverse_of(t[0:1, 0:ROWS]))
        rows = pl.ds(d * ROWS, ROWS)
        out[0, rows, :] = (a[0].astype(F32) * inv * weight).astype(BF16)
        out[1, rows, :] = a[1]
        if d == 0:
            rows = pl.ds(BLOCK, ROWS)
            shared = head_at(q, SHARED).astype(F32) * inv * (head_at(gain, SHARED) * FOLD)
            out[0, rows, :] = shared.astype(BF16)
            out[1, rows, :] = head_at(do, SHARED)


def norm_keys_kernel(index, t0, t1, t2, t3, b0, b1, b2, b3, gain, out):
    weight = head_at(gain, index[0])
    shared = head_at(gain, SHARED)
    for d, (t, b) in enumerate(((t0, b0), (t1, b1), (t2, b2), (t3, b3))):
        inv = along_rows(inverse_of(t[1:2, 0:ROWS]))
        rows = pl.ds(d * ROWS, ROWS)
        out[0, rows, :] = (b[0].astype(F32) * inv * weight).astype(BF16)
        out[1, rows, :] = b[1]
        out[2, rows, :] = (b[2].astype(F32) * inv * shared).astype(BF16)
        out[3, rows, :] = b[3]


STAT_KEYS = 256
BACK_KEYS = 512
BACK_QUERIES = 384


def unit_stats(queries, grads, keys, out, unit):
    high = jnp.full((1, BLOCK), -1e30, F32)
    total = jnp.zeros((1, BLOCK), F32)
    weighted = jnp.zeros((1, BLOCK), F32)
    for ref, base in keys:

        def step(j, carry):
            high, total, weighted = carry
            rows = pl.ds(pl.multiple_of(j * STAT_KEYS, STAT_KEYS), STAT_KEYS)
            s = dot(ref[base, rows, :], queries, NT)
            g = dot(ref[base + 1, rows, :], grads, NT)
            top = jnp.maximum(high, jnp.max(s, axis=0, keepdims=True))
            factor = jnp.exp2(high - top)
            w = jnp.exp2(s - top)
            return (
                top,
                total * factor + jnp.sum(w, axis=0, keepdims=True),
                weighted * factor + jnp.sum(w * g, axis=0, keepdims=True),
            )

        high, total, weighted = lax.fori_loop(
            0, BLOCK // STAT_KEYS, step, (high, total, weighted), unroll=True
        )
    cols = slice(unit * BLOCK, (unit + 1) * BLOCK)
    out[0:1, cols] = high + jnp.log2(total)
    out[1:2, cols] = weighted / total


def stats_kernel(index, y0, y1, y2, y3, x0, x1, out, shared):
    blocks = (y0, y1, y2, y3)
    for e, y in enumerate(blocks):
        shared[0, e * ROWS : (e + 1) * ROWS, :] = y[0, BLOCK:, :]
        shared[1, e * ROWS : (e + 1) * ROWS, :] = y[1, BLOCK:, :]
    for e, y in enumerate(blocks):
        unit_stats(y[0, 0:BLOCK, :], y[1, 0:BLOCK, :], ((x0, 0), (x1, 0)), out, e)
    unit_stats(shared[0], shared[1], ((x0, 2), (x1, 2)), out, 4)


def merge(parts):
    high = parts[0][0]
    for log, _ in parts[1:]:
        high = jnp.maximum(high, log)
    total = weighted = 0.0
    for log, delta in parts:
        w = jnp.exp2(log - high)
        total = total + w
        weighted = weighted + w * delta
    return high + jnp.log2(total), weighted / total


def back_kernel(
    index, s0, s1, s2, s3, y0, y1, y2, y3, x0, x1, u0, u1, u2, u3, w0, w1, shared, stat, dqt, keyt
):
    blocks = (y0, y1, y2, y3)
    stats = (s0, s1, s2, s3)
    for e, y in enumerate(blocks):
        shared[0, e * ROWS : (e + 1) * ROWS, :] = y[0, BLOCK:, :]
        shared[1, e * ROWS : (e + 1) * ROWS, :] = y[1, BLOCK:, :]
    for unit in range(5):
        parts = []
        for e, s in enumerate(stats):
            if unit < 4:
                at = (unit - e) % 4 * BLOCK
                parts.append((s[0:1, at : at + BLOCK], s[1:2, at : at + BLOCK]))
            else:
                turned = []
                for row in (0, 1):
                    cells = []
                    for f in range(4):
                        at = 4 * BLOCK + (f - e) % 4 * ROWS
                        cells.append(s[row : row + 1, at : at + ROWS])
                    turned.append(jnp.concatenate(cells, axis=1))
                parts.append(tuple(turned))
        log, delta = merge(parts)
        stat[0:1, unit * BLOCK : (unit + 1) * BLOCK] = log
        stat[1:2, unit * BLOCK : (unit + 1) * BLOCK] = delta
    dqt[...] = jnp.zeros_like(dqt)
    for group in range(2):
        base = 2 - 2 * group
        units = (4,) if group == 0 else (0, 1, 2, 3)
        for x, w in ((x1, w1), (x0, w0)):
            keyt[...] = x[base].T

            def step(j, _):
                rows = pl.ds(pl.multiple_of(j * BACK_KEYS_, BACK_KEYS_), BACK_KEYS_)
                kk = x[base, rows, :]
                vv = x[base + 1, rows, :]
                dk = jnp.zeros((BACK_KEYS_, HD), F32)
                dv = jnp.zeros((BACK_KEYS_, HD), F32)
                for unit in units:
                    for part in range(BLOCK // BACK_QUERIES):
                        cols = slice(part * BACK_QUERIES, (part + 1) * BACK_QUERIES)
                        source = shared if unit == 4 else blocks[unit]
                        qq = source[0, cols, :]
                        dd = source[1, cols, :]
                        at = slice(
                            unit * BLOCK + part * BACK_QUERIES,
                            unit * BLOCK + (part + 1) * BACK_QUERIES,
                        )
                        p = jnp.exp2(dot(kk, qq, NT) - stat[0:1, at])
                        ds = (p * (dot(vv, dd, NT) - stat[1:2, at])).astype(BF16)
                        dk = dk + dot(ds, qq, NN)
                        dv = dv + dot(p.astype(BF16), dd, NN)
                        dqt[:, at] += dot(keyt[:, rows], ds, NN)
                w[base, rows, :] = (dk * LN2).astype(BF16)
                w[base + 1, rows, :] = dv.astype(BF16)
                return 0

            lax.fori_loop(0, BLOCK // BACK_KEYS_, step, 0)
    for e, u in enumerate((u0, u1, u2, u3)):
        u[0:BLOCK, :] = (dqt[:, e * BLOCK : (e + 1) * BLOCK].T * SCALE).astype(BF16)
    whole = (dqt[:, 4 * BLOCK :].T * SCALE).astype(BF16)
    for e, u in enumerate((u0, u1, u2, u3)):
        u[BLOCK:, :] = whole[e * ROWS : (e + 1) * ROWS, :]


BACK_KEYS_ = 384


def reduce_kernel(
    index, u0, u1, u2, u3, w0, w1, y, x, z0, z1, z2, z3, own, inner
):
    inner[...] = jnp.zeros_like(inner)
    for d, z in enumerate((z0, z1, z2, z3)):
        rows = pl.ds(d * ROWS, ROWS)
        dq = sum(u[rows, :].astype(F32) for u in (u0, u1, u2, u3))
        grads = [w0[i, rows, :].astype(F32) + w1[i, rows, :].astype(F32) for i in range(4)]
        z[0] = dq.astype(BF16)
        for i in range(4):
            z[1 + i] = grads[i].astype(BF16)
        query = dq * y[0, rows, :].astype(F32) * (1.0 / FOLD)
        if d == 0:
            tail = pl.ds(BLOCK, ROWS)
            dq_shared = sum(u[tail, :].astype(F32) for u in (u0, u1, u2, u3))
            own[...] = dq_shared
            query = query + dq_shared * y[0, tail, :].astype(F32) * (1.0 / FOLD)
        inner[2 * d : 2 * d + 1, :] = along_lanes(query)
        key = grads[0] * x[0, rows, :].astype(F32) + grads[2] * x[2, rows, :].astype(F32)
        inner[2 * d + 1 : 2 * d + 2, :] = along_lanes(key)


def finish_kernel(
    index, tot, i0, i1, i2, i3, z0, z1, z2, z3, own, q, k, gain_q, gain_k, grad_q, grad_k, grad_v
):
    inners = (i0, i1, i2, i3)
    pieces = (z0, z1, z2, z3)
    inv_q = along_rows(inverse_of(tot[0:1, 0:ROWS]))
    inv_k = along_rows(inverse_of(tot[1:2, 0:ROWS]))
    mean_q = sum(i[2 * d : 2 * d + 1, :] for d, i in enumerate(inners)) / FEATURES
    mean_k = sum(i[2 * d + 1 : 2 * d + 2, :] for d, i in enumerate(inners)) / FEATURES
    slope_q = inv_q * along_rows(mean_q)
    slope_k = inv_k * along_rows(mean_k)

    def result(ref, gain, head, inv, slope, gradient):
        return (
            inv * (gradient * head_at(gain, head) - head_at(ref, head).astype(F32) * slope)
        ).astype(BF16)

    for d, z in enumerate(pieces):
        head = lax.rem(index[0] + d, 4)
        cols = pl.ds(pl.multiple_of(head * HD, HD), HD)
        grad_q[:, cols] = result(q, gain_q, head, inv_q, slope_q, z[0].astype(F32))
        grad_k[:, cols] = result(k, gain_k, head, inv_k, slope_k, z[1].astype(F32))
        grad_v[:, cols] = z[2]
    cols = slice(SHARED * HD, (SHARED + 1) * HD)
    dk = sum(z[3].astype(F32) for z in pieces)
    dv = sum(z[4].astype(F32) for z in pieces)
    grad_q[:, cols] = result(q, gain_q, SHARED, inv_q, slope_q, own[...])
    grad_k[:, cols] = result(k, gain_k, SHARED, inv_k, slope_k, dk)
    grad_v[:, cols] = dv.astype(BF16)


def cross_kernel(index, tot, qc, do, kt, vt, gain_c, gain_t, dq, inner, p0, p1, p2, p3, dkv):
    inv_c = along_rows(inverse_of(tot[2:3, 0:ROWS]))
    inv_t = along_rows(inverse_of(tot[3:4, :]))
    products = jnp.zeros((ROWS, HD), F32)
    for head in range(HEADS_DEV):
        cols = slice(head * HD, (head + 1) * HD)
        qq = (qc[:, cols].astype(F32) * inv_c * (gain_c[:, cols] * FOLD)).astype(BF16)
        kk = (kt[:, cols].astype(F32) * inv_t * gain_t[:, cols]).astype(BF16)
        dd = do[:, cols]
        s = dot(kk, qq, NT)
        g = dot(vt[:, cols], dd, NT)
        w = jnp.exp2(s - jnp.max(s, axis=0, keepdims=True))
        total = 1.0 / jnp.sum(w, axis=0, keepdims=True)
        delta = jnp.sum(w * g, axis=0, keepdims=True) * total
        p = w * total
        ds = (p * (g - delta)).astype(BF16)
        dkv[0, :, cols] = (dot(ds, qq, NN) * LN2).astype(BF16)
        dkv[1, :, cols] = dot(p.astype(BF16), dd, NN).astype(BF16)
        grad = dot(kk.T, ds, NN).T * SCALE
        dq[:, cols] = grad
        products = products + grad * qq.astype(F32)
    inner[...] = jnp.zeros_like(inner)
    inner[0:1, 0:ROWS] = along_lanes(products) * (1.0 / FOLD)
    for d, p in enumerate((p0, p1, p2, p3)):
        at = pl.multiple_of(lax.rem(index[0] + d, 4) * HD, HD)
        p[...] = dkv[:, pl.ds(at, HD), :]


def scatter_y_kernel(index, p0, p1, p2, p3, o0, o1, o2, o3, whole):
    whole[...] = sum(p[...].astype(F32) for p in (p0, p1, p2, p3)).astype(BF16)
    for d, o in enumerate((o0, o1, o2, o3)):
        at = pl.multiple_of(lax.rem(index[2] + d, 4) * 32, 32)
        o[...] = whole[:, pl.ds(at, 32), :]


def scatter_x_kernel(index, p0, p1, p2, p3, o0, o1, whole):
    whole[...] = sum(p[...].astype(F32) for p in (p0, p1, p2, p3)).astype(BF16)
    for d, o in enumerate((o0, o1)):
        at = pl.multiple_of(lax.rem(index[1] + d, 2) * 16, 16)
        o[...] = whole[:, pl.ds(at, 16), :]


def text_rows(index):
    return pl.multiple_of(index[0] * 128 + index[2] * 32 + index[1] * 16, 16)


def text_inner_kernel(index, o0, o1, tot, kt, gain_t, inner_c, grads, inner, invs):
    grads[...] = o0[...].astype(F32) + o1[...].astype(F32)
    rows = pl.ds(text_rows(index), 16)
    invs[...] = along_rows(inverse_of(tot[3:4, :]))
    inv = invs[rows, :]
    products = jnp.zeros((16, HD), F32)
    for head in range(HEADS_DEV):
        cols = slice(head * HD, (head + 1) * HD)
        unit = kt[rows, cols].astype(F32) * inv
        products = products + grads[0, :, cols] * gain_t[:, cols] * unit
    inner[...] = inner_c[...]
    padded = jnp.concatenate([products, jnp.zeros((HD - 16, HD), F32)], axis=0)
    inner[1:2, 0:HD] = along_lanes(padded)


def text_finish_kernel(
    index, grads, total, tot, kt, gain_t, qc, gain_c, dq, out, grad_qc, invs
):
    rows = pl.ds(text_rows(index), 16)
    invs[...] = along_rows(inverse_of(tot[3:4, :]))
    inv = invs[rows, :]
    slope = inv * along_rows(total[1:2, 0:HD] / FEATURES)[0:16, :]
    inv_c = along_rows(inverse_of(tot[2:3, 0:ROWS]))
    slope_c = inv_c * along_rows(total[0:1, 0:ROWS] / FEATURES)
    for head in range(HEADS_DEV):
        cols = slice(head * HD, (head + 1) * HD)
        scaled = grads[0, :, cols] * gain_t[:, cols]
        out[0, :, cols] = (inv * (scaled - kt[rows, cols].astype(F32) * slope)).astype(BF16)
        out[1, :, cols] = grads[1, :, cols].astype(BF16)
        scaled = dq[:, cols] * gain_c[:, cols]
        grad_qc[:, cols] = (inv_c * (scaled - qc[:, cols].astype(F32) * slope_c)).astype(BF16)


def gather_x_kernel(index, o0, o1, out):
    for d, o in enumerate((o0, o1)):
        at = pl.multiple_of(lax.rem(index[1] + d, 2) * 16, 16)
        out[:, pl.ds(at, 16), :] = o[...]


def gather_y_kernel(index, o0, o1, o2, o3, out):
    for d, o in enumerate((o0, o1, o2, o3)):
        at = pl.multiple_of(lax.rem(index[2] + 4 - d, 4) * 32, 32)
        out[:, pl.ds(at, 32), :] = o[...]


def gather_z_kernel(index, o0, o1, o2, o3, key, value):
    for d, o in enumerate((o0, o1, o2, o3)):
        at = pl.multiple_of(lax.rem(index[0] + 4 - d, 4) * 128, 128)
        key[pl.ds(at, 128), :] = o[0]
        value[pl.ds(at, 128), :] = o[1]


def shift(array, axis, by):
    size = lax.axis_size(axis)
    return lax.ppermute(array, axis, [(i, (i + by) % size) for i in range(size)])


def sum_tp(array):
    array = array + shift(array, "core", 1)
    return array + shift(array, "x_hi", 1)


def local(q, k, v, do, qc, doc, kt, vt, gain_q, gain_k, gain_c, gain_t):
    index = jnp.stack([lax.axis_index("z"), lax.axis_index("x_lo"), lax.axis_index("y")])
    index = index.astype(jnp.int32)
    gain_q, gain_k, gain_c, gain_t = (g.reshape(1, -1) for g in (gain_q, gain_k, gain_c, gain_t))
    head = shape((2, ROWS, HD))
    pair = shape((4, ROWS, HD))
    made = call(
        prepare_kernel,
        [shape((8, TEXT), F32)] + [head] * 4 + [pair] * 4,
        index,
        (q, k, v, do, qc, kt),
    )
    a = list(made[1:5])
    b = list(made[5:9])
    for d in (1, 3, 2):
        a[d] = shift(a[d], "z", d)
    tot = sum_tp(made[0])
    for d in (1, 3, 2):
        b[d] = shift(b[d], "z", d)
    tots = [tot] + [shift(tot, "z", d) for d in (1, 2, 3)]
    y0 = call(
        norm_queries_kernel,
        shape((2, BLOCK + ROWS, HD)),
        index,
        (*tots, *a, q, do, gain_q),
    )
    ys = [y0] + [shift(y0, "y", e) for e in (1, 2, 3)]
    x0 = call(norm_keys_kernel, shape((4, BLOCK, HD)), index, (*tots, *b, gain_k))
    x1 = shift(x0, "x_lo", 1)

    part = shape((2, TEXT // 4, HEADS_DEV * HD))
    dqc, inner_c, *parts = call(
        cross_kernel,
        [shape((ROWS, HEADS_DEV * HD), F32), shape((8, 256), F32)] + [part] * 4,
        index,
        (tot, qc, doc, kt, vt, gain_c, gain_t),
        scratch=[pltpu.VMEM((2, TEXT, HEADS_DEV * HD), BF16)],
        flops=2 * 5 * ROWS * TEXT * HEADS_DEV * HD * 2,
    )
    parts = [parts[0]] + [shift(parts[d], "z", d) for d in (1, 2, 3)]
    parts = call(
        scatter_y_kernel,
        [shape((2, 32, HEADS_DEV * HD))] * 4,
        index,
        parts,
        scratch=[pltpu.VMEM((2, 128, HEADS_DEV * HD), BF16)],
    )
    parts = [parts[0]] + [shift(parts[d], "y", d) for d in (1, 2, 3)]
    o0, o1 = call(
        scatter_x_kernel,
        [shape((2, 16, HEADS_DEV * HD))] * 2,
        index,
        parts,
        scratch=[pltpu.VMEM((2, 32, HEADS_DEV * HD), BF16)],
    )
    o1 = shift(o1, "x_lo", 1)
    tgrads, inner_ct = call(
        text_inner_kernel,
        [shape((2, 16, HEADS_DEV * HD), F32), shape((8, 256), F32)],
        index,
        (o0, o1, tot, kt, gain_t, inner_c),
        scratch=[pltpu.VMEM((TEXT, HD), F32)],
    )
    total_ct = sum_tp(inner_ct)
    o0, grad_qc = call(
        text_finish_kernel,
        [shape((2, 16, HEADS_DEV * HD)), shape((ROWS, HEADS_DEV * HD))],
        index,
        (tgrads, total_ct, tot, kt, gain_t, qc, gain_c, dqc),
        scratch=[pltpu.VMEM((TEXT, HD), F32)],
    )
    o0 = call(
        gather_x_kernel, shape((2, 32, HEADS_DEV * HD)), index, (o0, shift(o0, "x_lo", 1))
    )
    o0 = call(
        gather_y_kernel,
        shape((2, 128, HEADS_DEV * HD)),
        index,
        [o0] + [shift(o0, "y", d) for d in (1, 2, 3)],
    )
    grad_kt, grad_vt = call(
        gather_z_kernel,
        [shape((TEXT, HEADS_DEV * HD))] * 2,
        index,
        [o0] + [shift(o0, "z", d) for d in (1, 2, 3)],
    )

    area = 5 * BLOCK * 2 * BLOCK * HD * 2
    stats = call(
        stats_kernel,
        shape((2, 5 * BLOCK), F32),
        index,
        (*ys, x0, x1),
        scratch=[pltpu.VMEM((2, BLOCK, HD), BF16)],
        flops=area * 4,
    )
    stats = [stats] + [shift(stats, "y", e) for e in (1, 2, 3)]
    *us, w0, w1 = call(
        back_kernel,
        [shape((BLOCK + ROWS, HD))] * 4 + [shape((4, BLOCK, HD))] * 2,
        index,
        (*stats, *ys, x0, x1),
        scratch=[
            pltpu.VMEM((2, BLOCK, HD), BF16),
            pltpu.VMEM((2, 5 * BLOCK), F32),
            pltpu.VMEM((HD, 5 * BLOCK), F32),
            pltpu.VMEM((HD, BLOCK), BF16),
        ],
        flops=area * 10,
    )
    w1 = shift(w1, "x_lo", 1)
    us = [us[0]] + [shift(us[e], "y", -e) for e in (1, 2, 3)]
    *zs, own, inner = call(
        reduce_kernel,
        [shape((5, ROWS, HD))] * 4 + [shape((ROWS, HD), F32), shape((8, ROWS), F32)],
        index,
        (*us, w0, w1, y0, x0),
    )
    zs = [zs[0]] + [shift(zs[d], "z", -d) for d in (1, 2, 3)]
    inner = sum_tp(inner)
    inners = [inner] + [shift(inner, "z", -d) for d in (1, 2, 3)]
    wide = shape((ROWS, HEADS_DEV * HD))
    grad_q, grad_k, grad_v = call(
        finish_kernel,
        [wide] * 3,
        index,
        (tot, *inners, *zs, own, q, k, gain_q, gain_k),
    )
    return grad_q, grad_k, grad_v, grad_qc, grad_kt, grad_vt


def solution(mesh):
    fine = Mesh(mesh.devices.reshape(4, 2, 4, 2, 2), ("z", "x_lo", "y", "x_hi", "core"))
    ctx = ("z", "x_lo", "y")
    tp = ("x_hi", "core")
    in_specs = (P(ctx, tp),) * 6 + (P(None, tp),) * 2 + (P(tp),) * 4
    out_specs = (P(ctx, tp),) * 4 + (P(None, tp),) * 2
    return jax.shard_map(local, mesh=fine, in_specs=in_specs, out_specs=out_specs, check_vma=False)
```

```python
import math

import jax
import jax.numpy as jnp
from jax import lax
from jax.experimental import pallas as pl
from jax.experimental.pallas import tpu as pltpu
from jax.sharding import Mesh, PartitionSpec as P

HD = 128
ROWS = 192
FEATURES = 2560
HEADS_DEV = 5
SHARED = HEADS_DEV - 1
BLOCK = 4 * ROWS
TEXT = 512
EPS = 1e-6
SCALE = HD ** (-0.5)
FOLD = SCALE * math.log2(math.e)
LN2 = math.log(2.0)
F32 = jnp.float32
BF16 = jnp.bfloat16
NT = (((1,), (1,)), ((), ()))
NN = (((1,), (0,)), ((), ()))

VMEM = pl.BlockSpec(memory_space=pltpu.VMEM)
SMEM = pl.BlockSpec(memory_space=pltpu.SMEM)
ANY = pl.BlockSpec(memory_space=pl.ANY)
GAIN_Q, GAIN_K, GAIN_C, GAIN_T = range(4)


def shape(dims, dtype=BF16):
    return jax.ShapeDtypeStruct(dims, dtype)


class Line:
    def __init__(self, index):
        self.index = index
        self.last = None

    def __call__(self, us, kernel, outs, arrays, scratch=(), after=()):
        after = [*after] if self.last is None else [self.last, *after]

        def body(index, *refs):
            kernel(index, *refs[len(after) :])

        results = pl.pallas_call(
            body,
            out_shape=outs,
            in_specs=[SMEM] + [ANY] * len(after) + [VMEM] * len(arrays),
            out_specs=[VMEM] * len(outs),
            scratch_shapes=list(scratch),
            compiler_params=pltpu.CompilerParams(vmem_limit_bytes=56 * 2**20),
            cost_estimate=pl.CostEstimate(
                flops=int(us * 1.15e9), bytes_accessed=int(us * 3.69e6), transcendentals=0
            ),
        )(self.index, *after, *arrays)
        self.last = results[-1]
        return results

    def hold(self, array):
        return pl.pallas_call(
            lambda token, given, out: None,
            out_shape=shape(array.shape, array.dtype),
            in_specs=[ANY, ANY],
            out_specs=ANY,
            input_output_aliases={1: 0},
            cost_estimate=pl.CostEstimate(flops=0, bytes_accessed=0, transcendentals=0),
        )(self.last, array)


def dot(a, b, dims):
    return lax.dot_general(a, b, dims, preferred_element_type=F32)


def along_lanes(tile):
    return jnp.sum(tile.T, axis=0, keepdims=True)


def along_rows(row):
    return jnp.broadcast_to(row, (HD, row.shape[1])).T


def inverse_of(square_sum):
    return lax.rsqrt(square_sum / FEATURES + EPS)


def head_at(ref, head):
    start = head * HD
    if not isinstance(head, int):
        start = pl.multiple_of(start, HD)
    return ref[:, pl.ds(start, HD)]


def gain_at(gains, which, head):
    start = head * HD
    if not isinstance(head, int):
        start = pl.multiple_of(start, HD)
    return gains[which : which + 1, pl.ds(start, HD)]


def square_rows(ref):
    tile = None
    for head in range(HEADS_DEV):
        part = head_at(ref, head).astype(F32)
        tile = part * part if tile is None else tile + part * part
    return along_lanes(tile)


def sums_kernel(index, q, k, v, do, qc, kt, p0, p1, p2, p3, sums):
    sums[...] = jnp.zeros_like(sums)
    sums[0:1, 0:ROWS] = square_rows(q)
    sums[1:2, 0:ROWS] = square_rows(k)
    sums[2:3, 0:ROWS] = square_rows(qc)
    sums[3:4, :] = square_rows(kt)
    for d, p in enumerate((p0, p1, p2, p3)):
        head = index[0] ^ d
        p[0] = head_at(do, head)
        p[1] = head_at(v, head)
        p[2] = head_at(v, SHARED)


def norm_kernel(index, s0, s1, s2, s3, q, k, gains, p0, p1, p2, p3, own, tot):
    tot[...] = (s0[...] + s1[...]) + (s2[...] + s3[...])
    inv_q = along_rows(inverse_of(tot[0:1, 0:ROWS]))
    inv_k = along_rows(inverse_of(tot[1:2, 0:ROWS]))

    def query(head):
        return (head_at(q, head).astype(F32) * inv_q * (gain_at(gains, GAIN_Q, head) * FOLD)).astype(BF16)

    def key(head):
        return (head_at(k, head).astype(F32) * inv_k * gain_at(gains, GAIN_K, head)).astype(BF16)

    shared = key(SHARED)
    for d, p in enumerate((p0, p1, p2, p3)):
        head = index[0] ^ d
        p[0] = query(head)
        p[1] = key(head)
        p[2] = shared
    own[...] = query(SHARED)


def assemble_kernel(index, g0, g1, g2, g3, n0, n1, n2, n3, own, do, x, y):
    for d, (g, n) in enumerate(((g0, n0), (g1, n1), (g2, n2), (g3, n3))):
        rows = pl.ds(d * ROWS, ROWS)
        y[0, rows, :] = n[0]
        y[1, rows, :] = g[0]
        x[0, rows, :] = n[1]
        x[1, rows, :] = g[1]
        x[2, rows, :] = n[2]
        x[3, rows, :] = g[2]
    y[0, pl.ds(BLOCK, ROWS), :] = own[...]
    y[1, pl.ds(BLOCK, ROWS), :] = head_at(do, SHARED)


STAT_KEYS = 256
BACK_KEYS = 768
BACK_QUERIES = 256


def unit_stats(queries, grads, keys, out, unit):
    high = jnp.full((1, BLOCK), -1e30, F32)
    total = jnp.zeros((1, BLOCK), F32)
    weighted = jnp.zeros((1, BLOCK), F32)
    for ref, base in keys:

        def step(j, carry):
            high, total, weighted = carry
            rows = pl.ds(pl.multiple_of(j * STAT_KEYS, STAT_KEYS), STAT_KEYS)
            s = dot(ref[base, rows, :], queries, NT)
            g = dot(ref[base + 1, rows, :], grads, NT)
            top = jnp.maximum(high, jnp.max(s, axis=0, keepdims=True))
            factor = jnp.exp2(high - top)
            w = jnp.exp2(s - top)
            return (
                top,
                total * factor + jnp.sum(w, axis=0, keepdims=True),
                weighted * factor + jnp.sum(w * g, axis=0, keepdims=True),
            )

        high, total, weighted = lax.fori_loop(
            0, BLOCK // STAT_KEYS, step, (high, total, weighted), unroll=True
        )
    cols = slice(unit * BLOCK, (unit + 1) * BLOCK)
    out[0:1, cols] = high + jnp.log2(total)
    out[1:2, cols] = weighted / total


def gather_shared(blocks, shared):
    for e, y in enumerate(blocks):
        shared[0, e * ROWS : (e + 1) * ROWS, :] = y[0, BLOCK:, :]
        shared[1, e * ROWS : (e + 1) * ROWS, :] = y[1, BLOCK:, :]


def near_stats_kernel(index, y0, y1, y3, x0, x1, mine, theirs, o0, o1, o2, o3, out, whole):
    scatter_text(index, mine, theirs, (o0, o1, o2, o3), whole)
    for at, y in enumerate((y0, y1, y3)):
        unit_stats(y[0, 0:BLOCK, :], y[1, 0:BLOCK, :], ((x0, 0), (x1, 0)), out, at)


def far_stats_kernel(index, y0, y1, y2, y3, x0, x1, near, out, shared):
    out[:, 0 : 2 * BLOCK] = near[:, 0 : 2 * BLOCK]
    out[:, 3 * BLOCK : 4 * BLOCK] = near[:, 2 * BLOCK :]
    gather_shared((y0, y1, y2, y3), shared)
    unit_stats(y2[0, 0:BLOCK, :], y2[1, 0:BLOCK, :], ((x0, 0), (x1, 0)), out, 2)
    unit_stats(shared[0], shared[1], ((x0, 2), (x1, 2)), out, 4)


def merge(parts):
    high = parts[0][0]
    for log, _ in parts[1:]:
        high = jnp.maximum(high, log)
    total = weighted = 0.0
    for log, delta in parts:
        w = jnp.exp2(log - high)
        total = total + w
        weighted = weighted + w * delta
    return high + jnp.log2(total), weighted / total


def merge_stats(stats, stat):
    for unit in range(5):
        parts = []
        for e, s in enumerate(stats):
            if unit < 4:
                at = (unit ^ e) * BLOCK
                parts.append((s[0:1, at : at + BLOCK], s[1:2, at : at + BLOCK]))
            else:
                turned = []
                for row in (0, 1):
                    cells = []
                    for f in range(4):
                        at = 4 * BLOCK + (f ^ e) * ROWS
                        cells.append(s[row : row + 1, at : at + ROWS])
                    turned.append(jnp.concatenate(cells, axis=1))
                parts.append(tuple(turned))
        log, delta = merge(parts)
        stat[0:1, unit * BLOCK : (unit + 1) * BLOCK] = log
        stat[1:2, unit * BLOCK : (unit + 1) * BLOCK] = delta


def units_back(queries, stat_at, stat, key, value, keyt, dqt, store):
    keyt[...] = key[...].T

    def step(j, _):
        rows = pl.ds(pl.multiple_of(j * BACK_KEYS, BACK_KEYS), BACK_KEYS)
        kk = key[rows, :]
        vv = value[rows, :]
        dk = jnp.zeros((BACK_KEYS, HD), F32)
        dv = jnp.zeros((BACK_KEYS, HD), F32)
        for unit, (qref, dref) in enumerate(queries):
            for part in range(BLOCK // BACK_QUERIES):
                cols = slice(part * BACK_QUERIES, (part + 1) * BACK_QUERIES)
                qq = qref[cols, :]
                dd = dref[cols, :]
                at = stat_at[unit] * BLOCK + part * BACK_QUERIES
                at = slice(at, at + BACK_QUERIES)
                p = jnp.exp2(dot(kk, qq, NT) - stat[0:1, at])
                ds = (p * (dot(vv, dd, NT) - stat[1:2, at])).astype(BF16)
                dk = dk + dot(ds, qq, NN)
                dv = dv + dot(p.astype(BF16), dd, NN)
                dqt[:, at] += dot(keyt[:, rows], ds, NN)
        store[0, rows, :] = (dk * LN2).astype(BF16)
        store[1, rows, :] = dv.astype(BF16)
        return 0

    lax.fori_loop(0, BLOCK // BACK_KEYS, step, 0)


def back_queries(blocks, shared):
    return [(y.at[0], y.at[1]) for y in blocks], [(shared.at[0], shared.at[1])]


def back_away_kernel(
    index, s0, s1, s2, s3, y0, y1, y2, y3, x, w, dqt, stat, shared, keyt
):
    blocks = (y0, y1, y2, y3)
    merge_stats((s0, s1, s2, s3), stat)
    gather_shared(blocks, shared)
    dqt[...] = jnp.zeros_like(dqt)
    main, last = back_queries(blocks, shared)
    units_back(main, (0, 1, 2, 3), stat, x.at[0], x.at[1], keyt, dqt, w.at[0:2])
    units_back(last, (4,), stat, x.at[2], x.at[3], keyt, dqt, w.at[2:4])


def back_home_kernel(
    index, stat, y0, y1, y2, y3, x, before, w, u0, u1, u2, u3, dqt, shared, keyt
):
    blocks = (y0, y1, y2, y3)
    gather_shared(blocks, shared)
    dqt[...] = before[...]
    main, last = back_queries(blocks, shared)
    units_back(main, (0, 1, 2, 3), stat, x.at[0], x.at[1], keyt, dqt, w.at[0:2])
    units_back(last, (4,), stat, x.at[2], x.at[3], keyt, dqt, w.at[2:4])
    dq = (dqt[:, 4 * BLOCK :].T * SCALE).astype(BF16)
    for i, u in enumerate((u0, u1, u2, u3)):
        u[0:BLOCK, :] = (dqt[:, i * BLOCK : (i + 1) * BLOCK].T * SCALE).astype(BF16)
        u[BLOCK:, :] = dq[i * ROWS : (i + 1) * ROWS, :]


def reduce_keys_kernel(index, w0, w1, z0, z1, z2, z3):
    for d, z in enumerate((z0, z1, z2, z3)):
        rows = pl.ds(d * ROWS, ROWS)
        z[...] = (w0[:, rows, :].astype(F32) + w1[:, rows, :].astype(F32)).astype(BF16)


def reduce_queries_kernel(index, u0, u1, u2, u3, z0, z1, z2, z3, own):
    for d, z in enumerate((z0, z1, z2, z3)):
        rows = pl.ds(d * ROWS, ROWS)
        z[...] = sum(u[rows, :].astype(F32) for u in (u0, u1, u2, u3)).astype(BF16)
    own[...] = sum(u[BLOCK:, :].astype(F32) for u in (u0, u1, u2, u3))


def inner_kernel(
    index, tot, inner_c, inner_t, a0, a1, a2, a3, b0, b1, b2, b3, own, q, k, gains,
    grad_q, grad_k, grad_v, inner
):
    sum_q = jnp.zeros((ROWS, HD), F32)
    sum_k = jnp.zeros((ROWS, HD), F32)

    def add(total, x, which, head, gradient):
        return total + gradient * gain_at(gains, which, head) * head_at(x, head).astype(F32)

    for d, (a, b) in enumerate(((a0, b0), (a1, b1), (a2, b2), (a3, b3))):
        head = index[0] ^ d
        cols = pl.ds(pl.multiple_of(head * HD, HD), HD)
        dq = a[...].astype(F32)
        dk = b[0].astype(F32)
        sum_q = add(sum_q, q, GAIN_Q, head, dq)
        sum_k = add(sum_k, k, GAIN_K, head, dk)
        grad_q[:, cols] = dq
        grad_k[:, cols] = dk
        grad_v[:, cols] = b[1]
    cols = slice(SHARED * HD, (SHARED + 1) * HD)
    dk = sum(b[2].astype(F32) for b in (b0, b1, b2, b3))
    dv = sum(b[3].astype(F32) for b in (b0, b1, b2, b3))
    sum_q = add(sum_q, q, GAIN_Q, SHARED, own[...])
    sum_k = add(sum_k, k, GAIN_K, SHARED, dk)
    grad_q[:, cols] = own[...]
    grad_k[:, cols] = dk
    grad_v[:, cols] = dv.astype(BF16)
    inner[...] = jnp.zeros_like(inner)
    inner[0:1, 0:ROWS] = along_lanes(sum_q) * inverse_of(tot[0:1, 0:ROWS])
    inner[1:2, 0:ROWS] = along_lanes(sum_k) * inverse_of(tot[1:2, 0:ROWS])
    inner[2:3, 0:256] = inner_c[0:1, :]
    inner[3:4, :] = inner_t[0:1, :]


def finish_kernel(
    index, i0, i1, i2, i3, tot, q, k, qc, kt, dq, dk, dqc, dkt, gains,
    grad_q, grad_k, grad_qc, grad_kt
):
    mean = ((i0[...] + i1[...]) + (i2[...] + i3[...])) / FEATURES
    jobs = (
        (0, ROWS, q, dq, GAIN_Q, grad_q),
        (1, ROWS, k, dk, GAIN_K, grad_k),
        (2, ROWS, qc, dqc, GAIN_C, grad_qc),
        (3, TEXT, kt, dkt, GAIN_T, grad_kt),
    )
    for row, count, x, gradient, gain, out in jobs:
        inverse = inverse_of(tot[row : row + 1, 0:count])
        inv = along_rows(inverse)
        slope = along_rows(inverse * mean[row : row + 1, 0:count])
        for head in range(HEADS_DEV):
            cols = slice(head * HD, (head + 1) * HD)
            scaled = gradient[:, cols].astype(F32) * gain_at(gains, gain, head)
            out[:, cols] = (inv * (scaled - x[:, cols].astype(F32) * slope)).astype(BF16)


def cross_kernel(index, tot, qc, do, kt, vt, gains, keep, send, dq, inner, dkv):
    inv_c = along_rows(inverse_of(tot[2:3, 0:ROWS]))
    inv_t = along_rows(inverse_of(tot[3:4, :]))
    products = jnp.zeros((ROWS, HD), F32)
    for head in range(HEADS_DEV):
        cols = slice(head * HD, (head + 1) * HD)
        qq = (qc[:, cols].astype(F32) * inv_c * (gain_at(gains, GAIN_C, head) * FOLD)).astype(BF16)
        kk = (kt[:, cols].astype(F32) * inv_t * gain_at(gains, GAIN_T, head)).astype(BF16)
        dd = do[:, cols]
        s = dot(kk, qq, NT)
        g = dot(vt[:, cols], dd, NT)
        w = jnp.exp2(s - jnp.max(s, axis=0, keepdims=True))
        total = 1.0 / jnp.sum(w, axis=0, keepdims=True)
        delta = jnp.sum(w * g, axis=0, keepdims=True) * total
        p = w * total
        ds = (p * (g - delta)).astype(BF16)
        dkv[0, :, cols] = (dot(ds, qq, NN) * LN2).astype(BF16)
        dkv[1, :, cols] = dot(p.astype(BF16), dd, NN).astype(BF16)
        grad = dot(kk.T, ds, NN).T * SCALE
        dq[:, cols] = grad
        products = products + grad * qq.astype(F32)
    inner[...] = jnp.zeros_like(inner)
    inner[0:1, 0:ROWS] = along_lanes(products) * (1.0 / FOLD)
    half = text_half(index[0])
    keep[...] = dkv[:, pl.ds(pl.multiple_of(half * 256, 256), 256), :]
    send[...] = dkv[:, pl.ds(pl.multiple_of((1 - half) * 256, 256), 256), :]


def text_half(z):
    return (z ^ (z >> 1)) & 1


def scatter_text(index, mine, theirs, outs, whole):
    whole[...] = (mine[...].astype(F32) + theirs[...].astype(F32)).astype(BF16)
    for d, o in enumerate(outs):
        at = pl.multiple_of((index[2] ^ d) * 64, 64)
        o[...] = whole[:, pl.ds(at, 64), :]


def sum_text_kernel(index, p0, p1, p2, p3, out):
    out[...] = sum(p[...].astype(F32) for p in (p0, p1, p2, p3)).astype(BF16)


def gather_y_kernel(index, o0, o1, o2, o3, out):
    for d, o in enumerate((o0, o1, o2, o3)):
        at = pl.multiple_of((index[2] ^ d) * 64, 64)
        out[:, pl.ds(at, 64), :] = o[...]


def gather_z_kernel(index, o0, o1, tot, kt, gains, key, value, inner):
    half = text_half(index[0])
    for o, place in ((o0, half), (o1, 1 - half)):
        rows = pl.ds(pl.multiple_of(place * 256, 256), 256)
        key[rows, :] = o[0]
        value[rows, :] = o[1]
    inner[...] = jnp.zeros_like(inner)
    products = jnp.zeros((TEXT, HD), F32)
    for head in range(HEADS_DEV):
        scaled = head_at(key, head).astype(F32) * gain_at(gains, GAIN_T, head)
        products = products + scaled * head_at(kt, head).astype(F32)
    inner[0:1, :] = along_lanes(products) * inverse_of(tot[3:4, :])


def flip(array, axis, by):
    return lax.ppermute(array, axis, [(i, i ^ by) for i in range(lax.axis_size(axis))])


def over_tp(array):
    return flips([array] * 4, ("x_hi", "core"))


def flips(arrays, axis):
    return [arrays[0]] + [flip(arrays[d], axis, d) for d in range(1, len(arrays))]


def local(q, k, v, do, qc, doc, kt, vt, gain_q, gain_k, gain_c, gain_t):
    index = jnp.stack([lax.axis_index("z"), lax.axis_index("x_lo"), lax.axis_index("y")])
    line = Line(index.astype(jnp.int32))
    gains = jnp.concatenate([gain_q, gain_k, gain_c, gain_t]).reshape(4, -1)
    wide = shape((ROWS, HEADS_DEV * HD))
    text = HEADS_DEV * HD
    triple = shape((3, ROWS, HD))
    *gs, sums = line(
        2.5,
        sums_kernel, [triple] * 4 + [shape((8, TEXT), F32)], (q, k, v, do, qc, kt)
    )
    sums = over_tp(sums)
    gs = flips(gs, "z")
    *ns, own, tot = line(
        2.2,
        norm_kernel,
        [triple] * 4 + [shape((ROWS, HD)), shape((8, TEXT), F32)],
        (*sums, q, k, gains),
    )
    ns = flips(ns, "z")

    keep, send, dqc, inner_c = line(
        6.4,
        cross_kernel,
        [shape((2, TEXT // 2, text))] * 2 + [shape((ROWS, text), F32), shape((8, 256), F32)],
        (tot, qc, doc, kt, vt, gains),
        scratch=[pltpu.VMEM((2, TEXT, text), BF16)],
    )

    x0, y0 = line(
        2.5,
        assemble_kernel, [shape((4, BLOCK, HD)), shape((2, BLOCK + ROWS, HD))], (*gs, *ns, own, do)
    )
    ys = flips([y0] * 4, "y")
    x1 = flip(x0, "x_lo", 1)
    got = flip(line.hold(send), "z", 1)
    piece = shape((2, 64, text))
    *parts, near = line(
        8.5,
        near_stats_kernel,
        [piece] * 4 + [shape((2, 3 * BLOCK), F32)],
        (ys[0], ys[1], ys[3], x0, x1, keep, got),
        scratch=[pltpu.VMEM((2, TEXT // 2, text), BF16)],
    )
    parts = flips(parts, "y")
    block = pltpu.VMEM((2, BLOCK, HD), BF16)
    (stats,) = line(
        6.3,
        far_stats_kernel,
        [shape((2, 5 * BLOCK), F32)],
        (*ys, x0, x1, near),
        scratch=[block],
    )
    stats = flips([stats] * 4, "y")
    (part,) = line(1.7, sum_text_kernel, [piece], parts)
    parts = [part] + [flip(part, ("z", "x_lo"), by) for by in (1, 6, 7)]
    keyt = pltpu.VMEM((HD, BLOCK), BF16)
    quad = shape((4, BLOCK, HD))
    w1, dqt, stat = line(
        10.5,
        back_away_kernel,
        [quad, shape((HD, 5 * BLOCK), F32), shape((2, 5 * BLOCK), F32)],
        (*stats, *ys, x1),
        scratch=[block, keyt],
    )
    w1 = flip(w1, "x_lo", 1)
    (part,) = line(1.7, sum_text_kernel, [piece], parts)
    parts = flips([part] * 4, "y")
    w0, *us = line(
        10.5,
        back_home_kernel,
        [quad] + [shape((BLOCK + ROWS, HD))] * 4,
        (stat, *ys, x0, dqt),
        scratch=[pltpu.VMEM((HD, 5 * BLOCK), F32), block, keyt],
    )
    us = flips(us, "y")
    (part,) = line(1.8, gather_y_kernel, [shape((2, TEXT // 2, text))], parts)
    got = flip(part, "z", 1)
    bs = line(2, reduce_keys_kernel, [shape((4, ROWS, HD))] * 4, (w0, w1))
    bs = flips(bs, "z")
    *cs, own = line(
        2,
        reduce_queries_kernel,
        [shape((ROWS, HD))] * 4 + [shape((ROWS, HD), F32)],
        us,
        after=bs[1:2],
    )
    cs = flips(cs, "z")
    dkt, grad_vt, inner_t = line(
        2.7,
        gather_z_kernel,
        [shape((TEXT, text))] * 2 + [shape((8, TEXT), F32)],
        (part, got, tot, kt, gains),
    )
    whole = shape((ROWS, text), F32)
    dq, dk, grad_v, inner = line(
        2.7,
        inner_kernel,
        [whole, whole, wide, shape((8, TEXT), F32)],
        (tot, inner_c, inner_t, *cs, *bs, own, q, k, gains),
    )
    grad_q, grad_k, grad_qc, grad_kt = line(
        3.8,
        finish_kernel,
        [wide, wide, wide, shape((TEXT, text))],
        (*over_tp(inner), tot, q, k, qc, kt, dq, dk, dqc, dkt, gains),
    )
    return grad_q, grad_k, grad_v, grad_qc, grad_kt, grad_vt


def solution(mesh):
    fine = Mesh(mesh.devices.reshape(4, 2, 4, 2, 2), ("z", "x_lo", "y", "x_hi", "core"))
    ctx = ("z", "x_lo", "y")
    tp = ("x_hi", "core")
    in_specs = (P(ctx, tp),) * 6 + (P(None, tp),) * 2 + (P(tp),) * 4
    out_specs = (P(ctx, tp),) * 4 + (P(None, tp),) * 2
    return jax.shard_map(local, mesh=fine, in_specs=in_specs, out_specs=out_specs, check_vma=False)
```

```python
import math

import jax
import jax.numpy as jnp
from jax import lax
from jax.experimental import pallas as pl
from jax.experimental.pallas import tpu as pltpu
from jax.sharding import Mesh, PartitionSpec as P

HD = 128
ROWS = 192
FEATURES = 2560
HEADS_DEV = 5
SHARED = HEADS_DEV - 1
BLOCK = 4 * ROWS
TEXT = 512
EPS = 1e-6
SCALE = HD ** (-0.5)
FOLD = SCALE * math.log2(math.e)
LN2 = math.log(2.0)
F32 = jnp.float32
BF16 = jnp.bfloat16
NT = (((1,), (1,)), ((), ()))
NN = (((1,), (0,)), ((), ()))

VMEM = pl.BlockSpec(memory_space=pltpu.VMEM)
SMEM = pl.BlockSpec(memory_space=pltpu.SMEM)
ANY = pl.BlockSpec(memory_space=pl.ANY)
GAIN_Q, GAIN_K, GAIN_C, GAIN_T = range(4)


def shape(dims, dtype=BF16):
    return jax.ShapeDtypeStruct(dims, dtype)


class Line:
    def __init__(self, index):
        self.index = index
        self.last = None

    def __call__(self, us, kernel, outs, arrays, scratch=(), after=()):
        after = [*after] if self.last is None else [self.last, *after]

        def body(index, *refs):
            kernel(index, *refs[len(after) :])

        results = pl.pallas_call(
            body,
            out_shape=outs,
            in_specs=[SMEM] + [ANY] * len(after) + [VMEM] * len(arrays),
            out_specs=[VMEM] * len(outs),
            scratch_shapes=list(scratch),
            compiler_params=pltpu.CompilerParams(vmem_limit_bytes=56 * 2**20),
            cost_estimate=pl.CostEstimate(
                flops=int(us * 1.15e9), bytes_accessed=int(us * 3.69e6), transcendentals=0
            ),
        )(self.index, *after, *arrays)
        self.last = results[-1]
        return results

    def hold(self, array):
        return pl.pallas_call(
            lambda token, given, out: None,
            out_shape=shape(array.shape, array.dtype),
            in_specs=[ANY, ANY],
            out_specs=ANY,
            input_output_aliases={1: 0},
            cost_estimate=pl.CostEstimate(flops=0, bytes_accessed=0, transcendentals=0),
        )(self.last, array)


def dot(a, b, dims):
    return lax.dot_general(a, b, dims, preferred_element_type=F32)


def along_lanes(tile):
    return jnp.sum(tile.T, axis=0, keepdims=True)


def along_rows(row):
    return jnp.broadcast_to(row, (HD, row.shape[1])).T


def inverse_of(square_sum):
    return lax.rsqrt(square_sum / FEATURES + EPS)


def head_at(ref, head):
    start = head * HD
    if not isinstance(head, int):
        start = pl.multiple_of(start, HD)
    return ref[:, pl.ds(start, HD)]


def gain_at(gains, which, head):
    start = head * HD
    if not isinstance(head, int):
        start = pl.multiple_of(start, HD)
    return gains[which : which + 1, pl.ds(start, HD)]


def square_rows(ref):
    tile = None
    for head in range(HEADS_DEV):
        part = head_at(ref, head).astype(F32)
        tile = part * part if tile is None else tile + part * part
    return along_lanes(tile)


def sums_kernel(index, q, k, v, do, qc, kt, p0, p1, p2, p3, sums):
    sums[...] = jnp.zeros_like(sums)
    sums[0:1, 0:ROWS] = square_rows(q)
    sums[1:2, 0:ROWS] = square_rows(k)
    sums[2:3, 0:ROWS] = square_rows(qc)
    sums[3:4, :] = square_rows(kt)
    for d, p in enumerate((p0, p1, p2, p3)):
        head = index[0] ^ d
        p[0] = head_at(do, head)
        p[1] = head_at(v, head)
        p[2] = head_at(v, SHARED)


def norm_kernel(index, s0, s1, s2, s3, q, k, gains, p0, p1, p2, p3, own, tot):
    tot[...] = (s0[...] + s1[...]) + (s2[...] + s3[...])
    inv_q = along_rows(inverse_of(tot[0:1, 0:ROWS]))
    inv_k = along_rows(inverse_of(tot[1:2, 0:ROWS]))

    def query(head):
        return (head_at(q, head).astype(F32) * inv_q * (gain_at(gains, GAIN_Q, head) * FOLD)).astype(BF16)

    def key(head):
        return (head_at(k, head).astype(F32) * inv_k * gain_at(gains, GAIN_K, head)).astype(BF16)

    shared = key(SHARED)
    for d, p in enumerate((p0, p1, p2, p3)):
        head = index[0] ^ d
        p[0] = query(head)
        p[1] = key(head)
        p[2] = shared
    own[...] = query(SHARED)


def assemble_kernel(index, g0, g1, g2, g3, n0, n1, n2, n3, own, do, x, y):
    for d, (g, n) in enumerate(((g0, n0), (g1, n1), (g2, n2), (g3, n3))):
        rows = pl.ds(d * ROWS, ROWS)
        y[0, rows, :] = n[0]
        y[1, rows, :] = g[0]
        x[0, rows, :] = n[1]
        x[1, rows, :] = g[1]
        x[2, rows, :] = n[2]
        x[3, rows, :] = g[2]
    y[0, pl.ds(BLOCK, ROWS), :] = own[...]
    y[1, pl.ds(BLOCK, ROWS), :] = head_at(do, SHARED)


STAT_KEYS = 128
BACK_KEYS = 768
BACK_QUERIES = 768


def unit_stats(queries, grads, keys, out, unit):
    high = jnp.full((1, BLOCK), -1e30, F32)
    total = jnp.zeros((1, BLOCK), F32)
    weighted = jnp.zeros((1, BLOCK), F32)
    for ref, base in keys:

        def step(j, carry):
            high, total, weighted = carry
            rows = pl.ds(pl.multiple_of(j * STAT_KEYS, STAT_KEYS), STAT_KEYS)
            s = dot(ref[base, rows, :], queries, NT)
            g = dot(ref[base + 1, rows, :], grads, NT)
            top = jnp.maximum(high, jnp.max(s, axis=0, keepdims=True))
            factor = jnp.exp2(high - top)
            w = jnp.exp2(s - top)
            return (
                top,
                total * factor + jnp.sum(w, axis=0, keepdims=True),
                weighted * factor + jnp.sum(w * g, axis=0, keepdims=True),
            )

        high, total, weighted = lax.fori_loop(
            0, BLOCK // STAT_KEYS, step, (high, total, weighted), unroll=True
        )
    cols = slice(unit * BLOCK, (unit + 1) * BLOCK)
    out[0:1, cols] = high + jnp.log2(total)
    out[1:2, cols] = weighted / total


def gather_shared(blocks, shared):
    for e, y in enumerate(blocks):
        shared[0, e * ROWS : (e + 1) * ROWS, :] = y[0, BLOCK:, :]
        shared[1, e * ROWS : (e + 1) * ROWS, :] = y[1, BLOCK:, :]


def own_stats_kernel(index, y0, x0, out):
    unit_stats(y0[0, 0:BLOCK, :], y0[1, 0:BLOCK, :], ((x0, 0),), out, 0)


def near_stats_kernel(
    index, own, y0, y1, y3, x0, x1, mine, theirs, o0, o1, o2, o3, out, whole
):
    scatter_text(index, mine, theirs, (o0, o1, o2, o3), whole)
    unit_stats(y0[0, 0:BLOCK, :], y0[1, 0:BLOCK, :], ((x1, 0),), out, 0)
    cols = slice(0, BLOCK)
    log, delta = merge([(part[0:1, cols], part[1:2, cols]) for part in (own, out)])
    out[0:1, cols] = log
    out[1:2, cols] = delta
    for at, y in ((1, y1), (2, y3)):
        unit_stats(y[0, 0:BLOCK, :], y[1, 0:BLOCK, :], ((x0, 0), (x1, 0)), out, at)


def far_stats_kernel(index, y0, y1, y2, y3, x0, x1, near, out, shared):
    out[:, 0 : 2 * BLOCK] = near[:, 0 : 2 * BLOCK]
    out[:, 3 * BLOCK : 4 * BLOCK] = near[:, 2 * BLOCK :]
    gather_shared((y0, y1, y2, y3), shared)
    unit_stats(y2[0, 0:BLOCK, :], y2[1, 0:BLOCK, :], ((x0, 0), (x1, 0)), out, 2)
    unit_stats(shared[0], shared[1], ((x0, 2), (x1, 2)), out, 4)


def merge(parts):
    high = parts[0][0]
    for log, _ in parts[1:]:
        high = jnp.maximum(high, log)
    total = weighted = 0.0
    for log, delta in parts:
        w = jnp.exp2(log - high)
        total = total + w
        weighted = weighted + w * delta
    return high + jnp.log2(total), weighted / total


def merge_stats(stats, stat):
    for unit in range(5):
        parts = []
        for e, s in enumerate(stats):
            if unit < 4:
                at = (unit ^ e) * BLOCK
                parts.append((s[0:1, at : at + BLOCK], s[1:2, at : at + BLOCK]))
            else:
                turned = []
                for row in (0, 1):
                    cells = []
                    for f in range(4):
                        at = 4 * BLOCK + (f ^ e) * ROWS
                        cells.append(s[row : row + 1, at : at + ROWS])
                    turned.append(jnp.concatenate(cells, axis=1))
                parts.append(tuple(turned))
        log, delta = merge(parts)
        stat[0:1, unit * BLOCK : (unit + 1) * BLOCK] = log
        stat[1:2, unit * BLOCK : (unit + 1) * BLOCK] = delta


def units_back(queries, stat_at, stat, key, value, keyt, dqt, store):
    keyt[...] = key[...].T

    def step(j, _):
        rows = pl.ds(pl.multiple_of(j * BACK_KEYS, BACK_KEYS), BACK_KEYS)
        kk = key[rows, :]
        vv = value[rows, :]
        dk = jnp.zeros((BACK_KEYS, HD), F32)
        dv = jnp.zeros((BACK_KEYS, HD), F32)
        for unit, (qref, dref) in enumerate(queries):
            for part in range(BLOCK // BACK_QUERIES):
                cols = slice(part * BACK_QUERIES, (part + 1) * BACK_QUERIES)
                qq = qref[cols, :]
                dd = dref[cols, :]
                at = stat_at[unit] * BLOCK + part * BACK_QUERIES
                at = slice(at, at + BACK_QUERIES)
                p = jnp.exp2(dot(kk, qq, NT) - stat[0:1, at])
                ds = (p * (dot(vv, dd, NT) - stat[1:2, at])).astype(BF16)
                dk = dk + dot(ds, qq, NN)
                dv = dv + dot(p.astype(BF16), dd, NN)
                dqt[:, at] += dot(keyt[:, rows], ds, NN)
        store[0, rows, :] = (dk * LN2).astype(BF16)
        store[1, rows, :] = dv.astype(BF16)
        return 0

    lax.fori_loop(0, BLOCK // BACK_KEYS, step, 0)


def back_queries(blocks, shared):
    return [(y.at[0], y.at[1]) for y in blocks], [(shared.at[0], shared.at[1])]


def back_away_kernel(
    index, s0, s1, s2, s3, y0, y1, y2, y3, x, w, dqt, stat, shared, keyt
):
    blocks = (y0, y1, y2, y3)
    merge_stats((s0, s1, s2, s3), stat)
    gather_shared(blocks, shared)
    dqt[...] = jnp.zeros_like(dqt)
    main, last = back_queries(blocks, shared)
    units_back(main, (0, 1, 2, 3), stat, x.at[0], x.at[1], keyt, dqt, w.at[0:2])
    units_back(last, (4,), stat, x.at[2], x.at[3], keyt, dqt, w.at[2:4])


def back_home_kernel(
    index, stat, y0, y1, y2, y3, x, before, w, u0, u1, u2, u3, dqt, shared, keyt
):
    blocks = (y0, y1, y2, y3)
    gather_shared(blocks, shared)
    dqt[...] = before[...]
    main, last = back_queries(blocks, shared)
    units_back(main, (0, 1, 2, 3), stat, x.at[0], x.at[1], keyt, dqt, w.at[0:2])
    units_back(last, (4,), stat, x.at[2], x.at[3], keyt, dqt, w.at[2:4])
    dq = (dqt[:, 4 * BLOCK :].T * SCALE).astype(BF16)
    for i, u in enumerate((u0, u1, u2, u3)):
        u[0:BLOCK, :] = (dqt[:, i * BLOCK : (i + 1) * BLOCK].T * SCALE).astype(BF16)
        u[BLOCK:, :] = dq[i * ROWS : (i + 1) * ROWS, :]


def reduce_keys_kernel(index, w0, w1, z0, z1, z2, z3):
    for d, z in enumerate((z0, z1, z2, z3)):
        rows = pl.ds(d * ROWS, ROWS)
        z[...] = (w0[:, rows, :].astype(F32) + w1[:, rows, :].astype(F32)).astype(BF16)


def reduce_queries_kernel(index, u0, u1, u2, u3, z0, z1, z2, z3, own):
    for d, z in enumerate((z0, z1, z2, z3)):
        rows = pl.ds(d * ROWS, ROWS)
        z[...] = sum(u[rows, :].astype(F32) for u in (u0, u1, u2, u3)).astype(BF16)
    own[...] = sum(u[BLOCK:, :].astype(F32) for u in (u0, u1, u2, u3))


def inner_kernel(
    index, tot, inner_c, inner_t, a0, a1, a2, a3, b0, b1, b2, b3, own, q, k, gains,
    grad_q, grad_k, grad_v, inner
):
    sum_q = jnp.zeros((ROWS, HD), F32)
    sum_k = jnp.zeros((ROWS, HD), F32)

    def add(total, x, which, head, gradient):
        return total + gradient * gain_at(gains, which, head) * head_at(x, head).astype(F32)

    for d, (a, b) in enumerate(((a0, b0), (a1, b1), (a2, b2), (a3, b3))):
        head = index[0] ^ d
        cols = pl.ds(pl.multiple_of(head * HD, HD), HD)
        dq = a[...].astype(F32)
        dk = b[0].astype(F32)
        sum_q = add(sum_q, q, GAIN_Q, head, dq)
        sum_k = add(sum_k, k, GAIN_K, head, dk)
        grad_q[:, cols] = dq
        grad_k[:, cols] = dk
        grad_v[:, cols] = b[1]
    cols = slice(SHARED * HD, (SHARED + 1) * HD)
    dk = sum(b[2].astype(F32) for b in (b0, b1, b2, b3))
    dv = sum(b[3].astype(F32) for b in (b0, b1, b2, b3))
    sum_q = add(sum_q, q, GAIN_Q, SHARED, own[...])
    sum_k = add(sum_k, k, GAIN_K, SHARED, dk)
    grad_q[:, cols] = own[...]
    grad_k[:, cols] = dk
    grad_v[:, cols] = dv.astype(BF16)
    inner[...] = jnp.zeros_like(inner)
    inner[0:1, 0:ROWS] = along_lanes(sum_q) * inverse_of(tot[0:1, 0:ROWS])
    inner[1:2, 0:ROWS] = along_lanes(sum_k) * inverse_of(tot[1:2, 0:ROWS])
    inner[2:3, 0:256] = inner_c[0:1, :]
    inner[3:4, :] = inner_t[0:1, :]


def finish_kernel(
    index, i0, i1, i2, i3, tot, q, k, qc, kt, dq, dk, dqc, dkt, gains,
    grad_q, grad_k, grad_qc, grad_kt
):
    mean = ((i0[...] + i1[...]) + (i2[...] + i3[...])) / FEATURES
    jobs = (
        (0, ROWS, q, dq, GAIN_Q, grad_q),
        (1, ROWS, k, dk, GAIN_K, grad_k),
        (2, ROWS, qc, dqc, GAIN_C, grad_qc),
        (3, TEXT, kt, dkt, GAIN_T, grad_kt),
    )
    for row, count, x, gradient, gain, out in jobs:
        inverse = inverse_of(tot[row : row + 1, 0:count])
        inv = along_rows(inverse)
        slope = along_rows(inverse * mean[row : row + 1, 0:count])
        for head in range(HEADS_DEV):
            cols = slice(head * HD, (head + 1) * HD)
            scaled = gradient[:, cols].astype(F32) * gain_at(gains, gain, head)
            out[:, cols] = (inv * (scaled - x[:, cols].astype(F32) * slope)).astype(BF16)


def cross_kernel(index, tot, qc, do, kt, vt, gains, keep, send, dq, inner, dkv):
    inv_c = along_rows(inverse_of(tot[2:3, 0:ROWS]))
    inv_t = along_rows(inverse_of(tot[3:4, :]))
    products = jnp.zeros((ROWS, HD), F32)
    for head in range(HEADS_DEV):
        cols = slice(head * HD, (head + 1) * HD)
        qq = (qc[:, cols].astype(F32) * inv_c * (gain_at(gains, GAIN_C, head) * FOLD)).astype(BF16)
        kk = (kt[:, cols].astype(F32) * inv_t * gain_at(gains, GAIN_T, head)).astype(BF16)
        dd = do[:, cols]
        s = dot(kk, qq, NT)
        g = dot(vt[:, cols], dd, NT)
        w = jnp.exp2(s - jnp.max(s, axis=0, keepdims=True))
        total = 1.0 / jnp.sum(w, axis=0, keepdims=True)
        delta = jnp.sum(w * g, axis=0, keepdims=True) * total
        p = w * total
        ds = (p * (g - delta)).astype(BF16)
        dkv[0, :, cols] = (dot(ds, qq, NN) * LN2).astype(BF16)
        dkv[1, :, cols] = dot(p.astype(BF16), dd, NN).astype(BF16)
        grad = dot(kk.T, ds, NN).T * SCALE
        dq[:, cols] = grad
        products = products + grad * qq.astype(F32)
    inner[...] = jnp.zeros_like(inner)
    inner[0:1, 0:ROWS] = along_lanes(products) * (1.0 / FOLD)
    half = text_half(index[0])
    keep[...] = dkv[:, pl.ds(pl.multiple_of(half * 256, 256), 256), :]
    send[...] = dkv[:, pl.ds(pl.multiple_of((1 - half) * 256, 256), 256), :]


def text_half(z):
    return (z ^ (z >> 1)) & 1


def scatter_text(index, mine, theirs, outs, whole):
    whole[...] = (mine[...].astype(F32) + theirs[...].astype(F32)).astype(BF16)
    for d, o in enumerate(outs):
        at = pl.multiple_of((index[2] ^ d) * 64, 64)
        o[...] = whole[:, pl.ds(at, 64), :]


def sum_text_kernel(index, p0, p1, p2, p3, out):
    out[...] = sum(p[...].astype(F32) for p in (p0, p1, p2, p3)).astype(BF16)


def gather_y_kernel(index, o0, o1, o2, o3, out):
    for d, o in enumerate((o0, o1, o2, o3)):
        at = pl.multiple_of((index[2] ^ d) * 64, 64)
        out[:, pl.ds(at, 64), :] = o[...]


def gather_z_kernel(index, o0, o1, tot, kt, gains, key, value, inner):
    half = text_half(index[0])
    for o, place in ((o0, half), (o1, 1 - half)):
        rows = pl.ds(pl.multiple_of(place * 256, 256), 256)
        key[rows, :] = o[0]
        value[rows, :] = o[1]
    inner[...] = jnp.zeros_like(inner)
    products = jnp.zeros((TEXT, HD), F32)
    for head in range(HEADS_DEV):
        scaled = head_at(key, head).astype(F32) * gain_at(gains, GAIN_T, head)
        products = products + scaled * head_at(kt, head).astype(F32)
    inner[0:1, :] = along_lanes(products) * inverse_of(tot[3:4, :])


def flip(array, axis, by):
    return lax.ppermute(array, axis, [(i, i ^ by) for i in range(lax.axis_size(axis))])


def over_tp(array):
    return flips([array] * 4, ("x_hi", "core"))


def flips(arrays, axis):
    return [arrays[0]] + [flip(arrays[d], axis, d) for d in range(1, len(arrays))]


def local(q, k, v, do, qc, doc, kt, vt, gain_q, gain_k, gain_c, gain_t):
    index = jnp.stack([lax.axis_index("z"), lax.axis_index("x_lo"), lax.axis_index("y")])
    line = Line(index.astype(jnp.int32))
    gains = jnp.concatenate([gain_q, gain_k, gain_c, gain_t]).reshape(4, -1)
    wide = shape((ROWS, HEADS_DEV * HD))
    text = HEADS_DEV * HD
    triple = shape((3, ROWS, HD))
    *gs, sums = line(
        2.5,
        sums_kernel, [triple] * 4 + [shape((8, TEXT), F32)], (q, k, v, do, qc, kt)
    )
    sums = over_tp(sums)
    gs = flips(gs, "z")
    *ns, own, tot = line(
        2.2,
        norm_kernel,
        [triple] * 4 + [shape((ROWS, HD)), shape((8, TEXT), F32)],
        (*sums, q, k, gains),
    )
    ns = flips(ns, "z")

    keep, send, dqc, inner_c = line(
        6.4,
        cross_kernel,
        [shape((2, TEXT // 2, text))] * 2 + [shape((ROWS, text), F32), shape((8, 256), F32)],
        (tot, qc, doc, kt, vt, gains),
        scratch=[pltpu.VMEM((2, TEXT, text), BF16)],
    )

    x0, y0 = line(
        2.5,
        assemble_kernel, [shape((4, BLOCK, HD)), shape((2, BLOCK + ROWS, HD))], (*gs, *ns, own, do)
    )
    ys = flips([y0] * 4, "y")
    x1 = flip(x0, "x_lo", 1)
    got = flip(line.hold(send), "z", 1)
    piece = shape((2, 64, text))
    (mine,) = line(2, own_stats_kernel, [shape((2, BLOCK), F32)], (ys[0], x0))
    *parts, near = line(
        7.5,
        near_stats_kernel,
        [piece] * 4 + [shape((2, 3 * BLOCK), F32)],
        (mine, ys[0], ys[1], ys[3], x0, x1, keep, got),
        scratch=[pltpu.VMEM((2, TEXT // 2, text), BF16)],
    )
    parts = flips(parts, "y")
    block = pltpu.VMEM((2, BLOCK, HD), BF16)
    (stats,) = line(
        6.3,
        far_stats_kernel,
        [shape((2, 5 * BLOCK), F32)],
        (*ys, x0, x1, near),
        scratch=[block],
    )
    stats = flips([stats] * 4, "y")
    (part,) = line(1.7, sum_text_kernel, [piece], parts)
    parts = [part] + [flip(part, ("z", "x_lo"), by) for by in (1, 6, 7)]
    (part,) = line(1.7, sum_text_kernel, [piece], parts)
    parts = flips([part] * 4, "y")
    keyt = pltpu.VMEM((HD, BLOCK), BF16)
    quad = shape((4, BLOCK, HD))
    w1, dqt, stat = line(
        10.5,
        back_away_kernel,
        [quad, shape((HD, 5 * BLOCK), F32), shape((2, 5 * BLOCK), F32)],
        (*stats, *ys, x1),
        scratch=[block, keyt],
    )
    w1 = flip(w1, "x_lo", 1)
    (part,) = line(1.8, gather_y_kernel, [shape((2, TEXT // 2, text))], parts)
    got = flip(part, "z", 1)
    w0, *us = line(
        10.5,
        back_home_kernel,
        [quad] + [shape((BLOCK + ROWS, HD))] * 4,
        (stat, *ys, x0, dqt),
        scratch=[pltpu.VMEM((HD, 5 * BLOCK), F32), block, keyt],
    )
    us = flips(us, "y")
    bs = line(2, reduce_keys_kernel, [shape((4, ROWS, HD))] * 4, (w0, w1))
    bs = flips(bs, "z")
    dkt, grad_vt, inner_t = line(
        2.7,
        gather_z_kernel,
        [shape((TEXT, text))] * 2 + [shape((8, TEXT), F32)],
        (part, got, tot, kt, gains),
    )
    *cs, own = line(
        2,
        reduce_queries_kernel,
        [shape((ROWS, HD))] * 4 + [shape((ROWS, HD), F32)],
        us,
        after=bs[1:2],
    )
    cs = flips(cs, "z")
    whole = shape((ROWS, text), F32)
    dq, dk, grad_v, inner = line(
        2.7,
        inner_kernel,
        [whole, whole, wide, shape((8, TEXT), F32)],
        (tot, inner_c, inner_t, *cs, *bs, own, q, k, gains),
    )
    grad_q, grad_k, grad_qc, grad_kt = line(
        3.8,
        finish_kernel,
        [wide, wide, wide, shape((TEXT, text))],
        (*over_tp(inner), tot, q, k, qc, kt, dq, dk, dqc, dkt, gains),
    )
    return grad_q, grad_k, grad_v, grad_qc, grad_kt, grad_vt


def solution(mesh):
    fine = Mesh(mesh.devices.reshape(4, 2, 4, 2, 2), ("z", "x_lo", "y", "x_hi", "core"))
    ctx = ("z", "x_lo", "y")
    tp = ("x_hi", "core")
    in_specs = (P(ctx, tp),) * 6 + (P(None, tp),) * 2 + (P(tp),) * 4
    out_specs = (P(ctx, tp),) * 4 + (P(None, tp),) * 2
    return jax.shard_map(local, mesh=fine, in_specs=in_specs, out_specs=out_specs, check_vma=False)
```

```python
import math

import jax
import jax.numpy as jnp
from jax import lax
from jax.experimental import pallas as pl
from jax.experimental.pallas import tpu as pltpu
from jax.sharding import Mesh, PartitionSpec as P

HD = 128
ROWS = 192
FEATURES = 2560
HEADS_DEV = 5
SHARED = HEADS_DEV - 1
BLOCK = 4 * ROWS
TEXT = 512
EPS = 1e-6
SCALE = HD ** (-0.5)
FOLD = SCALE * math.log2(math.e)
LN2 = math.log(2.0)
F32 = jnp.float32
BF16 = jnp.bfloat16
NT = (((1,), (1,)), ((), ()))
NN = (((1,), (0,)), ((), ()))

VMEM = pl.BlockSpec(memory_space=pltpu.VMEM)
SMEM = pl.BlockSpec(memory_space=pltpu.SMEM)
ANY = pl.BlockSpec(memory_space=pl.ANY)
GAIN_Q, GAIN_K, GAIN_C, GAIN_T = range(4)


def shape(dims, dtype=BF16):
    return jax.ShapeDtypeStruct(dims, dtype)


class Line:
    def __init__(self, index):
        self.index = index
        self.last = None

    def __call__(self, us, kernel, outs, arrays, scratch=(), after=()):
        after = [*after] if self.last is None else [self.last, *after]

        def body(index, *refs):
            kernel(index, *refs[len(after) :])

        results = pl.pallas_call(
            body,
            out_shape=outs,
            in_specs=[SMEM] + [ANY] * len(after) + [VMEM] * len(arrays),
            out_specs=[VMEM] * len(outs),
            scratch_shapes=list(scratch),
            compiler_params=pltpu.CompilerParams(vmem_limit_bytes=56 * 2**20),
            cost_estimate=pl.CostEstimate(
                flops=int(us * 1.15e9), bytes_accessed=int(us * 3.69e6), transcendentals=0
            ),
        )(self.index, *after, *arrays)
        self.last = results[-1]
        return results

    def hold(self, array):
        return pl.pallas_call(
            lambda token, given, out: None,
            out_shape=shape(array.shape, array.dtype),
            in_specs=[ANY, ANY],
            out_specs=ANY,
            input_output_aliases={1: 0},
            cost_estimate=pl.CostEstimate(flops=0, bytes_accessed=0, transcendentals=0),
        )(self.last, array)


def dot(a, b, dims):
    return lax.dot_general(a, b, dims, preferred_element_type=F32)


def along_lanes(tile):
    return jnp.sum(tile.T, axis=0, keepdims=True)


def along_rows(row):
    return jnp.broadcast_to(row, (HD, row.shape[1])).T


def inverse_of(square_sum):
    return lax.rsqrt(square_sum / FEATURES + EPS)


def head_at(ref, head):
    start = head * HD
    if not isinstance(head, int):
        start = pl.multiple_of(start, HD)
    return ref[:, pl.ds(start, HD)]


def gain_at(gains, which, head):
    start = head * HD
    if not isinstance(head, int):
        start = pl.multiple_of(start, HD)
    return gains[which : which + 1, pl.ds(start, HD)]


def square_rows(ref):
    tile = None
    for head in range(HEADS_DEV):
        part = head_at(ref, head).astype(F32)
        tile = part * part if tile is None else tile + part * part
    return along_lanes(tile)


def sums_kernel(index, q, k, v, do, qc, kt, p0, p1, p2, p3, sums):
    sums[...] = jnp.zeros_like(sums)
    sums[0:1, 0:ROWS] = square_rows(q)
    sums[1:2, 0:ROWS] = square_rows(k)
    sums[2:3, 0:ROWS] = square_rows(qc)
    sums[3:4, :] = square_rows(kt)
    for d, p in enumerate((p0, p1, p2, p3)):
        head = index[0] ^ d
        p[0] = head_at(do, head)
        p[1] = head_at(v, head)
        p[2] = head_at(v, SHARED)


def norm_kernel(index, s0, s1, s2, s3, q, k, gains, p0, p1, p2, p3, own, tot):
    tot[...] = (s0[...] + s1[...]) + (s2[...] + s3[...])
    inv_q = along_rows(inverse_of(tot[0:1, 0:ROWS]))
    inv_k = along_rows(inverse_of(tot[1:2, 0:ROWS]))

    def query(head):
        return (head_at(q, head).astype(F32) * inv_q * (gain_at(gains, GAIN_Q, head) * FOLD)).astype(BF16)

    def key(head):
        return (head_at(k, head).astype(F32) * inv_k * gain_at(gains, GAIN_K, head)).astype(BF16)

    shared = key(SHARED)
    for d, p in enumerate((p0, p1, p2, p3)):
        head = index[0] ^ d
        p[0] = query(head)
        p[1] = key(head)
        p[2] = shared
    own[...] = query(SHARED)


def assemble_kernel(index, g0, g1, g2, g3, n0, n1, n2, n3, own, do, x, y):
    for d, (g, n) in enumerate(((g0, n0), (g1, n1), (g2, n2), (g3, n3))):
        rows = pl.ds(d * ROWS, ROWS)
        y[0, rows, :] = n[0]
        y[1, rows, :] = g[0]
        x[0, rows, :] = n[1]
        x[1, rows, :] = g[1]
        x[2, rows, :] = n[2]
        x[3, rows, :] = g[2]
    y[0, pl.ds(BLOCK, ROWS), :] = own[...]
    y[1, pl.ds(BLOCK, ROWS), :] = head_at(do, SHARED)


STAT_KEYS = 128
BACK_KEYS = 768
BACK_QUERIES = 768


def unit_stats(queries, grads, keys, out, unit):
    high = jnp.full((1, BLOCK), -1e30, F32)
    total = jnp.zeros((1, BLOCK), F32)
    weighted = jnp.zeros((1, BLOCK), F32)
    for ref, base in keys:

        def step(j, carry):
            high, total, weighted = carry
            rows = pl.ds(pl.multiple_of(j * STAT_KEYS, STAT_KEYS), STAT_KEYS)
            s = dot(ref[base, rows, :], queries, NT)
            g = dot(ref[base + 1, rows, :], grads, NT)
            top = jnp.maximum(high, jnp.max(s, axis=0, keepdims=True))
            factor = jnp.exp2(high - top)
            w = jnp.exp2(s - top)
            return (
                top,
                total * factor + jnp.sum(w, axis=0, keepdims=True),
                weighted * factor + jnp.sum(w * g, axis=0, keepdims=True),
            )

        high, total, weighted = lax.fori_loop(
            0, BLOCK // STAT_KEYS, step, (high, total, weighted), unroll=True
        )
    cols = slice(unit * BLOCK, (unit + 1) * BLOCK)
    out[0:1, cols] = high + jnp.log2(total)
    out[1:2, cols] = weighted / total


def gather_shared(blocks, shared):
    for e, y in enumerate(blocks):
        shared[0, e * ROWS : (e + 1) * ROWS, :] = y[0, BLOCK:, :]
        shared[1, e * ROWS : (e + 1) * ROWS, :] = y[1, BLOCK:, :]


def own_stats_kernel(index, y0, x0, out):
    unit_stats(y0[0, 0:BLOCK, :], y0[1, 0:BLOCK, :], ((x0, 0),), out, 0)


def near_stats_kernel(
    index, own, y0, y1, y3, x0, x1, mine, theirs, o0, o1, o2, o3, out, whole
):
    scatter_text(index, mine, theirs, (o0, o1, o2, o3), whole)
    unit_stats(y0[0, 0:BLOCK, :], y0[1, 0:BLOCK, :], ((x1, 0),), out, 0)
    cols = slice(0, BLOCK)
    log, delta = merge([(part[0:1, cols], part[1:2, cols]) for part in (own, out)])
    out[0:1, cols] = log
    out[1:2, cols] = delta
    for at, y in ((1, y1), (2, y3)):
        unit_stats(y[0, 0:BLOCK, :], y[1, 0:BLOCK, :], ((x0, 0), (x1, 0)), out, at)


def far_stats_kernel(index, y0, y1, y2, y3, x0, x1, near, out, shared):
    out[:, 0 : 2 * BLOCK] = near[:, 0 : 2 * BLOCK]
    out[:, 3 * BLOCK : 4 * BLOCK] = near[:, 2 * BLOCK :]
    gather_shared((y0, y1, y2, y3), shared)
    unit_stats(y2[0, 0:BLOCK, :], y2[1, 0:BLOCK, :], ((x0, 0), (x1, 0)), out, 2)
    unit_stats(shared[0], shared[1], ((x0, 2), (x1, 2)), out, 4)


def merge(parts):
    high = parts[0][0]
    for log, _ in parts[1:]:
        high = jnp.maximum(high, log)
    total = weighted = 0.0
    for log, delta in parts:
        w = jnp.exp2(log - high)
        total = total + w
        weighted = weighted + w * delta
    return high + jnp.log2(total), weighted / total


def merge_stats(stats, stat):
    for unit in range(5):
        parts = []
        for e, s in enumerate(stats):
            if unit < 4:
                at = (unit ^ e) * BLOCK
                parts.append((s[0:1, at : at + BLOCK], s[1:2, at : at + BLOCK]))
            else:
                turned = []
                for row in (0, 1):
                    cells = []
                    for f in range(4):
                        at = 4 * BLOCK + (f ^ e) * ROWS
                        cells.append(s[row : row + 1, at : at + ROWS])
                    turned.append(jnp.concatenate(cells, axis=1))
                parts.append(tuple(turned))
        log, delta = merge(parts)
        stat[0:1, unit * BLOCK : (unit + 1) * BLOCK] = log
        stat[1:2, unit * BLOCK : (unit + 1) * BLOCK] = delta


def units_back(queries, stat_at, stat, key, value, keyt, dqt, store):
    keyt[...] = key[...].T

    def step(j, _):
        rows = pl.ds(pl.multiple_of(j * BACK_KEYS, BACK_KEYS), BACK_KEYS)
        kk = key[rows, :]
        vv = value[rows, :]
        dk = jnp.zeros((BACK_KEYS, HD), F32)
        dv = jnp.zeros((BACK_KEYS, HD), F32)
        for unit, (qref, dref) in enumerate(queries):
            for part in range(BLOCK // BACK_QUERIES):
                cols = slice(part * BACK_QUERIES, (part + 1) * BACK_QUERIES)
                qq = qref[cols, :]
                dd = dref[cols, :]
                at = stat_at[unit] * BLOCK + part * BACK_QUERIES
                at = slice(at, at + BACK_QUERIES)
                p = jnp.exp2(dot(kk, qq, NT) - stat[0:1, at])
                ds = (p * (dot(vv, dd, NT) - stat[1:2, at])).astype(BF16)
                dk = dk + dot(ds, qq, NN)
                dv = dv + dot(p.astype(BF16), dd, NN)
                dqt[:, at] += dot(keyt[:, rows], ds, NN)
        store[0, rows, :] = (dk * LN2).astype(BF16)
        store[1, rows, :] = dv.astype(BF16)
        return 0

    lax.fori_loop(0, BLOCK // BACK_KEYS, step, 0)


def back_queries(blocks, shared):
    return [(y.at[0], y.at[1]) for y in blocks], [(shared.at[0], shared.at[1])]


def back_away_kernel(
    index, s0, s1, s2, s3, y0, y1, y2, y3, x, w, dqt, stat, shared, keyt
):
    blocks = (y0, y1, y2, y3)
    merge_stats((s0, s1, s2, s3), stat)
    gather_shared(blocks, shared)
    dqt[...] = jnp.zeros_like(dqt)
    main, last = back_queries(blocks, shared)
    units_back(main, (0, 1, 2, 3), stat, x.at[0], x.at[1], keyt, dqt, w.at[0:2])
    units_back(last, (4,), stat, x.at[2], x.at[3], keyt, dqt, w.at[2:4])


def back_home_kernel(
    index, stat, y0, y1, y2, y3, x, before, w, u0, u1, u2, u3, dqt, shared, keyt
):
    blocks = (y0, y1, y2, y3)
    gather_shared(blocks, shared)
    dqt[...] = before[...]
    main, last = back_queries(blocks, shared)
    units_back(main, (0, 1, 2, 3), stat, x.at[0], x.at[1], keyt, dqt, w.at[0:2])
    units_back(last, (4,), stat, x.at[2], x.at[3], keyt, dqt, w.at[2:4])
    dq = (dqt[:, 4 * BLOCK :].T * SCALE).astype(BF16)
    for i, u in enumerate((u0, u1, u2, u3)):
        u[0:BLOCK, :] = (dqt[:, i * BLOCK : (i + 1) * BLOCK].T * SCALE).astype(BF16)
        u[BLOCK:, :] = dq[i * ROWS : (i + 1) * ROWS, :]


def reduce_keys_kernel(index, w0, w1, z0, z1, z2, z3):
    for d, z in enumerate((z0, z1, z2, z3)):
        rows = pl.ds(d * ROWS, ROWS)
        z[...] = (w0[:, rows, :].astype(F32) + w1[:, rows, :].astype(F32)).astype(BF16)


def reduce_queries_kernel(index, u0, u1, u2, u3, z0, z1, z2, z3, own):
    for d, z in enumerate((z0, z1, z2, z3)):
        rows = pl.ds(d * ROWS, ROWS)
        z[...] = sum(u[rows, :].astype(F32) for u in (u0, u1, u2, u3)).astype(BF16)
    own[...] = sum(u[BLOCK:, :].astype(F32) for u in (u0, u1, u2, u3))


def inner_kernel(
    index, tot, inner_c, inner_t, a0, a1, a2, a3, b0, b1, b2, b3, own, q, k, gains,
    grad_q, grad_k, grad_v, inner
):
    sum_q = jnp.zeros((ROWS, HD), F32)
    sum_k = jnp.zeros((ROWS, HD), F32)

    def add(total, x, which, head, gradient):
        return total + gradient * gain_at(gains, which, head) * head_at(x, head).astype(F32)

    for d, (a, b) in enumerate(((a0, b0), (a1, b1), (a2, b2), (a3, b3))):
        head = index[0] ^ d
        cols = pl.ds(pl.multiple_of(head * HD, HD), HD)
        dq = a[...].astype(F32)
        dk = b[0].astype(F32)
        sum_q = add(sum_q, q, GAIN_Q, head, dq)
        sum_k = add(sum_k, k, GAIN_K, head, dk)
        grad_q[:, cols] = a[...]
        grad_k[:, cols] = b[0]
        grad_v[:, cols] = b[1]
    cols = slice(SHARED * HD, (SHARED + 1) * HD)
    dk = sum(b[2].astype(F32) for b in (b0, b1, b2, b3))
    dv = sum(b[3].astype(F32) for b in (b0, b1, b2, b3))
    sum_q = add(sum_q, q, GAIN_Q, SHARED, own[...])
    sum_k = add(sum_k, k, GAIN_K, SHARED, dk)
    grad_q[:, cols] = own[...].astype(BF16)
    grad_k[:, cols] = dk.astype(BF16)
    grad_v[:, cols] = dv.astype(BF16)
    inner[...] = jnp.zeros_like(inner)
    inner[0:1, 0:ROWS] = along_lanes(sum_q) * inverse_of(tot[0:1, 0:ROWS])
    inner[1:2, 0:ROWS] = along_lanes(sum_k) * inverse_of(tot[1:2, 0:ROWS])
    inner[2:3, 0:256] = inner_c[0:1, :]
    inner[3:4, :] = inner_t[0:1, :]


def finish_kernel(
    index, i0, i1, i2, i3, tot, q, k, qc, kt, dq, dk, dqc, dkt, gains,
    grad_q, grad_k, grad_qc, grad_kt
):
    mean = ((i0[...] + i1[...]) + (i2[...] + i3[...])) / FEATURES
    jobs = (
        (0, ROWS, q, dq, GAIN_Q, grad_q),
        (1, ROWS, k, dk, GAIN_K, grad_k),
        (2, ROWS, qc, dqc, GAIN_C, grad_qc),
        (3, TEXT, kt, dkt, GAIN_T, grad_kt),
    )
    for row, count, x, gradient, gain, out in jobs:
        inverse = inverse_of(tot[row : row + 1, 0:count])
        inv = along_rows(inverse)
        slope = along_rows(inverse * mean[row : row + 1, 0:count])
        for head in range(HEADS_DEV):
            cols = slice(head * HD, (head + 1) * HD)
            scaled = gradient[:, cols].astype(F32) * gain_at(gains, gain, head)
            out[:, cols] = (inv * (scaled - x[:, cols].astype(F32) * slope)).astype(BF16)


def cross_kernel(index, tot, qc, do, kt, vt, gains, keep, send, dq, inner, dkv):
    inv_c = along_rows(inverse_of(tot[2:3, 0:ROWS]))
    inv_t = along_rows(inverse_of(tot[3:4, :]))
    products = jnp.zeros((ROWS, HD), F32)
    for head in range(HEADS_DEV):
        cols = slice(head * HD, (head + 1) * HD)
        qq = (qc[:, cols].astype(F32) * inv_c * (gain_at(gains, GAIN_C, head) * FOLD)).astype(BF16)
        kk = (kt[:, cols].astype(F32) * inv_t * gain_at(gains, GAIN_T, head)).astype(BF16)
        dd = do[:, cols]
        s = dot(kk, qq, NT)
        g = dot(vt[:, cols], dd, NT)
        w = jnp.exp2(s - jnp.max(s, axis=0, keepdims=True))
        total = 1.0 / jnp.sum(w, axis=0, keepdims=True)
        delta = jnp.sum(w * g, axis=0, keepdims=True) * total
        p = w * total
        ds = (p * (g - delta)).astype(BF16)
        dkv[0, :, cols] = (dot(ds, qq, NN) * LN2).astype(BF16)
        dkv[1, :, cols] = dot(p.astype(BF16), dd, NN).astype(BF16)
        grad = dot(kk.T, ds, NN).T * SCALE
        dq[:, cols] = grad
        products = products + grad * qq.astype(F32)
    inner[...] = jnp.zeros_like(inner)
    inner[0:1, 0:ROWS] = along_lanes(products) * (1.0 / FOLD)
    half = text_half(index[0])
    keep[...] = dkv[:, pl.ds(pl.multiple_of(half * 256, 256), 256), :]
    send[...] = dkv[:, pl.ds(pl.multiple_of((1 - half) * 256, 256), 256), :]


def text_half(z):
    return (z ^ (z >> 1)) & 1


def scatter_text(index, mine, theirs, outs, whole):
    whole[...] = (mine[...].astype(F32) + theirs[...].astype(F32)).astype(BF16)
    for d, o in enumerate(outs):
        at = pl.multiple_of((index[2] ^ d) * 64, 64)
        o[...] = whole[:, pl.ds(at, 64), :]


def sum_text_kernel(index, p0, p1, p2, p3, out):
    out[...] = sum(p[...].astype(F32) for p in (p0, p1, p2, p3)).astype(BF16)


def gather_y_kernel(index, o0, o1, o2, o3, out):
    for d, o in enumerate((o0, o1, o2, o3)):
        at = pl.multiple_of((index[2] ^ d) * 64, 64)
        out[:, pl.ds(at, 64), :] = o[...]


def gather_z_kernel(index, o0, o1, tot, kt, gains, key, value, inner):
    half = text_half(index[0])
    for o, place in ((o0, half), (o1, 1 - half)):
        rows = pl.ds(pl.multiple_of(place * 256, 256), 256)
        key[rows, :] = o[0]
        value[rows, :] = o[1]
    inner[...] = jnp.zeros_like(inner)
    products = jnp.zeros((TEXT, HD), F32)
    for head in range(HEADS_DEV):
        scaled = head_at(key, head).astype(F32) * gain_at(gains, GAIN_T, head)
        products = products + scaled * head_at(kt, head).astype(F32)
    inner[0:1, :] = along_lanes(products) * inverse_of(tot[3:4, :])


def flip(array, axis, by):
    return lax.ppermute(array, axis, [(i, i ^ by) for i in range(lax.axis_size(axis))])


def over_tp(array):
    return flips([array] * 4, ("x_hi", "core"))


def flips(arrays, axis):
    return [arrays[0]] + [flip(arrays[d], axis, d) for d in range(1, len(arrays))]


def local(q, k, v, do, qc, doc, kt, vt, gain_q, gain_k, gain_c, gain_t):
    index = jnp.stack([lax.axis_index("z"), lax.axis_index("x_lo"), lax.axis_index("y")])
    line = Line(index.astype(jnp.int32))
    gains = jnp.concatenate([gain_q, gain_k, gain_c, gain_t]).reshape(4, -1)
    wide = shape((ROWS, HEADS_DEV * HD))
    text = HEADS_DEV * HD
    triple = shape((3, ROWS, HD))
    *gs, sums = line(
        2.5,
        sums_kernel, [triple] * 4 + [shape((8, TEXT), F32)], (q, k, v, do, qc, kt)
    )
    sums = over_tp(sums)
    gs = flips(gs, "z")
    *ns, own, tot = line(
        2.2,
        norm_kernel,
        [triple] * 4 + [shape((ROWS, HD)), shape((8, TEXT), F32)],
        (*sums, q, k, gains),
    )
    ns = flips(ns, "z")

    keep, send, dqc, inner_c = line(
        6.4,
        cross_kernel,
        [shape((2, TEXT // 2, text))] * 2 + [shape((ROWS, text), F32), shape((8, 256), F32)],
        (tot, qc, doc, kt, vt, gains),
        scratch=[pltpu.VMEM((2, TEXT, text), BF16)],
    )

    x0, y0 = line(
        2.5,
        assemble_kernel, [shape((4, BLOCK, HD)), shape((2, BLOCK + ROWS, HD))], (*gs, *ns, own, do)
    )
    ys = flips([y0] * 4, "y")
    x1 = flip(x0, "x_lo", 1)
    got = flip(line.hold(send), "z", 1)
    piece = shape((2, 64, text))
    (mine,) = line(2, own_stats_kernel, [shape((2, BLOCK), F32)], (ys[0], x0))
    *parts, near = line(
        7.5,
        near_stats_kernel,
        [piece] * 4 + [shape((2, 3 * BLOCK), F32)],
        (mine, ys[0], ys[1], ys[3], x0, x1, keep, got),
        scratch=[pltpu.VMEM((2, TEXT // 2, text), BF16)],
    )
    parts = flips(parts, "y")
    block = pltpu.VMEM((2, BLOCK, HD), BF16)
    (stats,) = line(
        6.3,
        far_stats_kernel,
        [shape((2, 5 * BLOCK), F32)],
        (*ys, x0, x1, near),
        scratch=[block],
    )
    stats = flips([stats] * 4, "y")
    (part,) = line(1.7, sum_text_kernel, [piece], parts)
    parts = [part] + [flip(part, ("z", "x_lo"), by) for by in (1, 6, 7)]
    (part,) = line(1.7, sum_text_kernel, [piece], parts)
    parts = flips([part] * 4, "y")
    keyt = pltpu.VMEM((HD, BLOCK), BF16)
    quad = shape((4, BLOCK, HD))
    w1, dqt, stat = line(
        10.5,
        back_away_kernel,
        [quad, shape((HD, 5 * BLOCK), F32), shape((2, 5 * BLOCK), F32)],
        (*stats, *ys, x1),
        scratch=[block, keyt],
    )
    w1 = flip(w1, "x_lo", 1)
    (part,) = line(1.8, gather_y_kernel, [shape((2, TEXT // 2, text))], parts)
    got = flip(part, "z", 1)
    w0, *us = line(
        10.5,
        back_home_kernel,
        [quad] + [shape((BLOCK + ROWS, HD))] * 4,
        (stat, *ys, x0, dqt),
        scratch=[pltpu.VMEM((HD, 5 * BLOCK), F32), block, keyt],
    )
    us = flips(us, "y")
    bs = line(2, reduce_keys_kernel, [shape((4, ROWS, HD))] * 4, (w0, w1))
    bs = flips(bs, "z")
    dkt, grad_vt, inner_t = line(
        2.7,
        gather_z_kernel,
        [shape((TEXT, text))] * 2 + [shape((8, TEXT), F32)],
        (part, got, tot, kt, gains),
    )
    *cs, own = line(
        2,
        reduce_queries_kernel,
        [shape((ROWS, HD))] * 4 + [shape((ROWS, HD), F32)],
        us,
        after=bs[1:2],
    )
    cs = flips(cs, "z")
    dq, dk, grad_v, inner = line(
        2.7,
        inner_kernel,
        [wide, wide, wide, shape((8, TEXT), F32)],
        (tot, inner_c, inner_t, *cs, *bs, own, q, k, gains),
    )
    grad_q, grad_k, grad_qc, grad_kt = line(
        3.8,
        finish_kernel,
        [wide, wide, wide, shape((TEXT, text))],
        (*over_tp(inner), tot, q, k, qc, kt, dq, dk, dqc, dkt, gains),
    )
    return grad_q, grad_k, grad_v, grad_qc, grad_kt, grad_vt


def solution(mesh):
    fine = Mesh(mesh.devices.reshape(4, 2, 4, 2, 2), ("z", "x_lo", "y", "x_hi", "core"))
    ctx = ("z", "x_lo", "y")
    tp = ("x_hi", "core")
    in_specs = (P(ctx, tp),) * 6 + (P(None, tp),) * 2 + (P(tp),) * 4
    out_specs = (P(ctx, tp),) * 4 + (P(None, tp),) * 2
    return jax.shard_map(local, mesh=fine, in_specs=in_specs, out_specs=out_specs, check_vma=False)
```
